128 devices in a mesh: lat: 4 (over z), lon: 32 (over y, x, core).
Axes of the slice: x: 4, y: 4, z: 4, core: 2. Of those that a mesh axis runs over, the one named last changes fastest.
Arguments:
- grid_feat: bfloat16 [262144, 512], P(('lat', 'lon')), may hold values from -6 to 6
- mesh_feat: bfloat16 [32768, 512], P(('lat', 'lon')), may hold values from -6 to 6
- g2m_src: int32 [524288], P(('lat', 'lon')), may hold values from 0 to 262143, as said below
- g2m_dst: int32 [524288], P(('lat', 'lon')), may hold values from 0 to 32767, as said below
- g2m_weight: float32 [524288], P(('lat', 'lon')), may hold values from 0.25 to 1.75
- mesh_src: int32 [128, 128, 32], P(('lat', 'lon')), may hold values from 0 to 32767, as said below
- mesh_dst: int32 [128, 128, 32], P(('lat', 'lon')), may hold values from 0 to 32767, as said below
- mesh_count: int32 [128, 128], P(('lat', 'lon')), may hold values from 1 to 32, as said below
- m2g_src: int32 [262144, 3], P(('lat', 'lon')), may hold values from 0 to 32767, as said below
- m2g_weight: float32 [262144, 3], P(('lat', 'lon')), may hold values from 0.25 to 1.75
- w_in: bfloat16 [512, 512], replicated, may hold values from -0.25 to 0.25
- w_enc: bfloat16 [512, 512], replicated, may hold values from -0.25 to 0.25
- w_send: bfloat16 [512, 512], replicated, may hold values from -0.25 to 0.25
- w_recv: bfloat16 [512, 512], replicated, may hold values from -0.25 to 0.25
- w_edge: bfloat16 [512, 512], replicated, may hold values from -0.25 to 0.25
- w_node: bfloat16 [512, 512], replicated, may hold values from -0.25 to 0.25
- w_dec: bfloat16 [512, 512], replicated, may hold values from -0.25 to 0.25
- w_out: bfloat16 [512, 512], replicated, may hold values from -0.25 to 0.25
- gain_enc: float32 [512], replicated, may hold values from 0.1 to 1.9
- gain_node: float32 [512], replicated, may hold values from 0.1 to 1.9
- gain_out: float32 [512], replicated, may hold values from 0.1 to 1.9
Outputs:
- grid_out: bfloat16 [262144, 512], P(('lat', 'lon'))
- mesh_out: bfloat16 [32768, 512], P(('lat', 'lon'))
The draws below stay inside these ranges and needn't reach their ends.
Inputs may be any that keep to these rules, and one draw needn't show every extreme that they name: `g2m_src`: the edges of tile t's shard have senders on tile t; every grid node of a tile sends at least one edge. `g2m_dst`: each receiver is owned by a tile at most one latitude band and one longitude sector (periodically) away from the sender's tile; bands do not wrap. mesh_src[s, t, k] is owned by tile s. mesh_dst[s, t, k] is owned by tile t. `mesh_count`: every tile pair has at least one live slot; some pairs fill all 32. `m2g_src`: each sender is owned by a tile at most one latitude band and one longitude sector (periodically) away from the grid node's tile; bands do not wrap.
All inputs are finite; a program needn't handle non-finite values.
Results may differ from the reference program's by a relative error of at most 0.013.
Values may be sent and summed in bfloat16 or wider, within the bound.
No kernel may reach another device: no remote copies, remote signals or barrier semaphores. Data moves between devices by JAX's collectives and lax.ppermute only.
A program may use at most 128 MiB of HBM per device.

```python
import jax
import jax.numpy as jnp
from jax import lax

D = 512
G_DEV = 2048
M_DEV = 256
E_G = 4096
CAP = 32
GRID = 262144
MESH = 32768
EDGES_G = 524288
N_LAT = 4
N_LON = 32
DEVICES = 128


def tile_near(key, home):
    key_lat, key_lon = jax.random.split(key)
    home_lat = home // N_LON
    home_lon = home % N_LON
    near_lat = home_lat + jax.random.randint(key_lat, home.shape, -1, 2)
    near_lat = jnp.where((near_lat < 0) | (near_lat >= N_LAT), home_lat, near_lat)
    near_lon = (home_lon + jax.random.randint(key_lon, home.shape, -1, 2)) % N_LON
    return (near_lat * N_LON + near_lon).astype(jnp.int32)


def draw_g2m_src(key, part):
    key = jax.random.fold_in(key, 11)
    edge_ids = jnp.arange(EDGES_G, dtype=jnp.int32)
    home = edge_ids // E_G
    within = edge_ids % E_G
    picked = jax.random.randint(key, (EDGES_G,), 0, G_DEV)
    local = jnp.where(within < G_DEV, within, picked)
    return (home * G_DEV + local).astype(jnp.int32)


def draw_g2m_dst(key, part):
    key = jax.random.fold_in(key, 12)
    key_tile, key_node = jax.random.split(key)
    home = jnp.arange(EDGES_G, dtype=jnp.int32) // E_G
    target = tile_near(key_tile, home)
    local = jax.random.randint(key_node, (EDGES_G,), 0, M_DEV)
    return (target * M_DEV + local).astype(jnp.int32)


def draw_mesh_count(key, part):
    key = jax.random.fold_in(key, 13)
    columns = jnp.broadcast_to(jnp.arange(DEVICES, dtype=jnp.int32)[None, :], (DEVICES, DEVICES))
    recv_lat = columns // N_LON
    polar = (recv_lat == 0) | (recv_lat == N_LAT - 1)
    base = jax.random.randint(key, (DEVICES, DEVICES), 1, max(CAP // 2, 1) + 1)
    return jnp.where(polar, CAP, base).astype(jnp.int32)


def draw_mesh_src(key, part):
    key = jax.random.fold_in(key, 14)
    owner = jnp.arange(DEVICES, dtype=jnp.int32)[:, None, None]
    local = jax.random.randint(key, (DEVICES, DEVICES, CAP), 0, M_DEV)
    return (owner * M_DEV + local).astype(jnp.int32)


def draw_mesh_dst(key, part):
    key = jax.random.fold_in(key, 15)
    owner = jnp.arange(DEVICES, dtype=jnp.int32)[None, :, None]
    local = jax.random.randint(key, (DEVICES, DEVICES, CAP), 0, M_DEV)
    return (owner * M_DEV + local).astype(jnp.int32)


def draw_m2g_src(key, part):
    key = jax.random.fold_in(key, 16)
    key_tile, key_node = jax.random.split(key)
    home = jnp.broadcast_to((jnp.arange(GRID, dtype=jnp.int32) // G_DEV)[:, None], (GRID, 3))
    target = tile_near(key_tile, home)
    local = jax.random.randint(key_node, (GRID, 3), 0, M_DEV)
    return (target * M_DEV + local).astype(jnp.int32)


def block_scale(own_key, extent, cuts, low, high):
    factor_of, own = 1.0, jax.random.fold_in(own_key, 6)
    for position, blocks in cuts:
        heights = jnp.exp(jax.random.uniform(jax.random.fold_in(own, position), (blocks,), jnp.float32, low / len(cuts), high / len(cuts)))
        factor_of = factor_of * jnp.repeat(heights, extent[position] // blocks).reshape([-1 if axis == position else 1 for axis in range(len(extent))])
    return factor_of


def noise(rng, dims, width, most, pieces=(), kind=jnp.bfloat16):
    loudness = block_scale(rng, dims, pieces, -0.22, 0.18) if pieces else 1.0
    result = jax.random.normal(rng, dims, jnp.float32) * width * loudness
    return jnp.minimum(jnp.maximum(result, -most), most).astype(kind)


def setup_inputs(seed: int = 0) -> dict:
    arg_keys = jax.random.split(jax.random.key(seed), 22)
    grid_feat = noise(arg_keys[0], (GRID, D), 1.0, 6.0, ((0, 128),))
    mesh_feat = noise(arg_keys[1], (MESH, D), 1.0, 6.0, ((0, 128),))
    g2m_src = draw_g2m_src(jax.random.fold_in(arg_keys[21], 71), 0)
    g2m_dst = draw_g2m_dst(jax.random.fold_in(arg_keys[21], 71), 0)
    g2m_weight = jnp.clip(0.25 + 1.5 * jax.random.uniform(arg_keys[4], (EDGES_G,), jnp.float32) ** block_scale(arg_keys[4], (EDGES_G,), ((0, 128),), -0.2, 0.2), 0.25, 1.75)
    mesh_src = draw_mesh_src(jax.random.fold_in(arg_keys[21], 71), 0)
    mesh_dst = draw_mesh_dst(jax.random.fold_in(arg_keys[21], 71), 0)
    mesh_count = draw_mesh_count(jax.random.fold_in(arg_keys[21], 71), 0)
    m2g_src = draw_m2g_src(jax.random.fold_in(arg_keys[21], 71), 0)
    m2g_weight = jnp.clip(0.25 + 1.5 * jax.random.uniform(arg_keys[9], (GRID, 3), jnp.float32) ** block_scale(arg_keys[9], (GRID, 3), ((0, 128),), -0.2, 0.2), 0.25, 1.75)
    w_in = noise(arg_keys[10], (D, D), D ** -0.5, 0.25)
    w_enc = noise(arg_keys[11], (D, D), D ** -0.5, 0.25)
    w_send = noise(arg_keys[12], (D, D), D ** -0.5, 0.25)
    w_recv = noise(arg_keys[13], (D, D), D ** -0.5, 0.25)
    w_edge = noise(arg_keys[14], (D, D), D ** -0.5, 0.25)
    w_node = noise(arg_keys[15], (D, D), D ** -0.5, 0.25)
    w_dec = noise(arg_keys[16], (D, D), D ** -0.5, 0.25)
    w_out = noise(arg_keys[17], (D, D), D ** -0.5, 0.25)
    gain_enc = jnp.clip(1.0 + 0.18 * jax.random.normal(arg_keys[18], (D,), jnp.float32), 0.1, 1.9)
    gain_node = jnp.clip(1.0 + 0.18 * jax.random.normal(arg_keys[19], (D,), jnp.float32), 0.1, 1.9)
    gain_out = jnp.clip(1.0 + 0.18 * jax.random.normal(arg_keys[20], (D,), jnp.float32), 0.1, 1.9)
    return {"grid_feat": grid_feat, "mesh_feat": mesh_feat, "g2m_src": g2m_src, "g2m_dst": g2m_dst, "g2m_weight": g2m_weight, "mesh_src": mesh_src, "mesh_dst": mesh_dst, "mesh_count": mesh_count, "m2g_src": m2g_src, "m2g_weight": m2g_weight, "w_in": w_in, "w_enc": w_enc, "w_send": w_send, "w_recv": w_recv, "w_edge": w_edge, "w_node": w_node, "w_dec": w_dec, "w_out": w_out, "gain_enc": gain_enc, "gain_node": gain_node, "gain_out": gain_out}


def layer_norm(values):
    center = values - lax.optimization_barrier(jnp.mean(values, axis=-1, keepdims=True))
    spread = lax.optimization_barrier(jnp.mean(center * center, axis=-1, keepdims=True))
    return center * lax.rsqrt(spread + 1e-05)

def reference(grid_feat, mesh_feat, g2m_src, g2m_dst, g2m_weight, mesh_src, mesh_dst, mesh_count, m2g_src, m2g_weight, w_in, w_enc, w_send, w_recv, w_edge, w_node, w_dec, w_out, gain_enc, gain_node, gain_out):
    hidden = jax.nn.silu(jnp.dot(grid_feat, w_in, preferred_element_type=jnp.float32)).astype(jnp.bfloat16)
    src_blocks = g2m_src.reshape(DEVICES, E_G)
    dst_blocks = g2m_dst.reshape(DEVICES, E_G)
    wgt_blocks = g2m_weight.reshape(DEVICES, E_G)

    def encode_step(totals, inputs):
        sender, target, weight = inputs
        message = (weight[:, None] * hidden[sender].astype(jnp.float32)).astype(jnp.bfloat16)
        return (totals.at[target].add(message.astype(jnp.float32)), None)
    pooled, _ = lax.scan(encode_step, jnp.zeros((MESH, D), jnp.float32), (src_blocks, dst_blocks, wgt_blocks))
    update = jax.nn.silu(jnp.dot(pooled.astype(jnp.bfloat16), w_enc, preferred_element_type=jnp.float32))
    first = (mesh_feat.astype(jnp.float32) + gain_enc * layer_norm(update)).astype(jnp.bfloat16)
    sent_proj = jnp.dot(first, w_send, preferred_element_type=jnp.float32).astype(jnp.bfloat16)
    recv_proj = jnp.dot(first, w_recv, preferred_element_type=jnp.float32)
    slot_iota = jnp.arange(CAP, dtype=jnp.int32)
    live_all = (slot_iota[None, None, :] < mesh_count[:, :, None]).reshape(DEVICES, DEVICES * CAP)

    def process_step(totals, inputs):
        sender, target, live = inputs
        joined = jax.nn.silu(sent_proj[sender].astype(jnp.float32) + recv_proj[target]).astype(jnp.bfloat16)
        edge_msg = jnp.dot(joined, w_edge, preferred_element_type=jnp.float32).astype(jnp.bfloat16)
        edge_msg = jnp.where(live[:, None], edge_msg, jnp.zeros_like(edge_msg))
        return (totals.at[target].add(edge_msg.astype(jnp.float32)), None)
    pooled_two, _ = lax.scan(process_step, jnp.zeros((MESH, D), jnp.float32), (mesh_src.reshape(DEVICES, DEVICES * CAP), mesh_dst.reshape(DEVICES, DEVICES * CAP), live_all))
    node_upd = jax.nn.silu(jnp.dot(pooled_two.astype(jnp.bfloat16), w_node, preferred_element_type=jnp.float32))
    mesh_out = (first.astype(jnp.float32) + gain_node * layer_norm(node_upd)).astype(jnp.bfloat16)
    decoded = jnp.dot(mesh_out, w_dec, preferred_element_type=jnp.float32).astype(jnp.bfloat16)
    gathered = m2g_weight[:, 0:1] * decoded[m2g_src[:, 0]].astype(jnp.float32)
    gathered = gathered + m2g_weight[:, 1:2] * decoded[m2g_src[:, 1]].astype(jnp.float32)
    gathered = gathered + m2g_weight[:, 2:3] * decoded[m2g_src[:, 2]].astype(jnp.float32)
    grid_upd = jax.nn.silu(jnp.dot(gathered.astype(jnp.bfloat16), w_out, preferred_element_type=jnp.float32))
    grid_out = (grid_feat.astype(jnp.float32) + gain_out * layer_norm(grid_upd)).astype(jnp.bfloat16)
    return (grid_out, mesh_out)
```

```python
import functools

import jax
import jax.numpy as jnp
from jax import lax
from jax.experimental import pallas as pl
from jax.experimental.pallas import tpu as pltpu
from jax.sharding import PartitionSpec as P

BF16 = jnp.bfloat16
F32 = jnp.float32
LANES = 128
VMEM_LIMIT = 56 * 1024 * 1024
VMEM = pltpu.VMEM
SMEM = pltpu.SMEM


def silu(v):
    half = 0.5 * v
    return half + half * jnp.tanh(half)


def layer_norm(values):
    center = values - jnp.mean(values, axis=-1, keepdims=True)
    spread = jnp.mean(center * center, axis=-1, keepdims=True)
    return center * lax.rsqrt(spread + 1e-05)


def whole(space=VMEM):
    return pl.BlockSpec(memory_space=space)


def scatter_kernel(src_ref, dst_ref, wgt_ref, grid_ref, w_ref, *refs, unroll):
    outs, (y_ref, acc_a, acc_b) = refs[:3], refs[3:]
    rows, latent = grid_ref.shape
    parts = latent // LANES
    step = 256

    def project(i, carry):
        base = pl.multiple_of(i * step, step)
        y = silu(jnp.dot(grid_ref[pl.ds(base, step), :], w_ref[...], preferred_element_type=F32))
        for j in range(parts):
            y_ref[pl.ds(base * parts + j, step, stride=parts), :] = y[:, j * LANES : (j + 1) * LANES]
        return carry

    lax.fori_loop(0, rows // step, project, 0)

    slots = acc_a.shape[0] // parts
    zero = jnp.zeros((step * parts, LANES), F32)

    def clear(i, carry):
        base = pl.multiple_of(i * step * parts, step * parts)
        acc_a[pl.ds(base, step * parts), :] = zero
        acc_b[pl.ds(base, step * parts), :] = zero
        return carry

    lax.fori_loop(0, slots // step, clear, 0)

    edges = src_ref.shape[0]

    def add_edges(i, carry):
        for u in range(unroll):
            e = i * unroll + u
            acc = (acc_a, acc_b)[u % 2]
            s = pl.multiple_of(src_ref[e], parts)
            d = pl.multiple_of(dst_ref[e], parts)
            acc[pl.ds(d, parts), :] += wgt_ref[e] * y_ref[pl.ds(s, parts), :]
        return carry

    lax.fori_loop(0, edges // unroll, add_edges, 0)

    for n, out in enumerate(outs):
        per = out.shape[0]

        def emit(i, carry, n=n, out=out, per=per):
            base = pl.multiple_of(i * step, step)
            for j in range(parts):
                rows_j = pl.ds((n * per + base) * parts + j, step, stride=parts)
                total = acc_a[rows_j, :] + acc_b[rows_j, :]
                out[pl.ds(base, step), j * LANES : (j + 1) * LANES] = total.astype(out.dtype)
            return carry

        lax.fori_loop(0, per // step, emit, 0)


def scatter(src4, dst4, weight, grid_feat, w_in, slots):
    rows, latent = grid_feat.shape
    parts = latent // LANES
    out = jax.ShapeDtypeStruct((slots // 3, latent), BF16)
    return pl.pallas_call(
        functools.partial(scatter_kernel, unroll=16),
        out_shape=(out, out, out),
        in_specs=[whole(SMEM)] * 3 + [whole()] * 2,
        out_specs=(whole(),) * 3,
        scratch_shapes=[
            pltpu.VMEM((rows * parts, LANES), F32),
            pltpu.VMEM((slots * parts, LANES), F32),
            pltpu.VMEM((slots * parts, LANES), F32),
        ],
        compiler_params=pltpu.CompilerParams(vmem_limit_bytes=VMEM_LIMIT),
        name="grid_to_mesh",
    )(src4, dst4, weight, grid_feat, w_in)


def node_kernel(src_ref, a_ref, b_ref, c_ref, mesh_ref, w_enc, w_send, w_recv, gain, first_ref, q_ref, rows_ref, p_ref):
    @pl.when(pl.program_id(0) == 0)
    def _():
        pooled = a_ref[...].astype(F32) + b_ref[...].astype(F32) + c_ref[...].astype(F32)
        update = silu(jnp.dot(pooled.astype(BF16), w_enc[...], preferred_element_type=F32))
        first = (mesh_ref[...].astype(F32) + gain[...] * layer_norm(update)).astype(BF16)
        first_ref[...] = first
        p_ref[...] = jnp.dot(first, w_send[...], preferred_element_type=F32).astype(BF16)
        q_ref[...] = jnp.dot(first, w_recv[...], preferred_element_type=F32).astype(BF16)

    block = rows_ref.shape[0]
    nodes = p_ref.shape[0]
    picks = src_ref[0]
    table = (lax.broadcasted_iota(jnp.int32, (nodes, block), 0) == picks).astype(BF16)
    rows_ref[...] = lax.dot_general(
        table, p_ref[...], (((0,), (0,)), ((), ())), preferred_element_type=F32
    ).astype(BF16)


def node_stage(src, a, b, c, mesh_feat, w_enc, w_send, w_recv, gain):
    nodes, latent = mesh_feat.shape
    edges = src.size
    block = 512
    full = pl.BlockSpec((nodes, latent), lambda i: (0, 0))
    weight = pl.BlockSpec((latent, latent), lambda i: (0, 0))
    vec = pl.BlockSpec((1, latent), lambda i: (0, 0))
    return pl.pallas_call(
        node_kernel,
        grid=(edges // block,),
        out_shape=(
            jax.ShapeDtypeStruct((nodes, latent), BF16),
            jax.ShapeDtypeStruct((nodes, latent), BF16),
            jax.ShapeDtypeStruct((edges, latent), BF16),
        ),
        in_specs=[pl.BlockSpec((1, 1, block), lambda i: (i, 0, 0)), full, full, full, full, weight, weight, weight, vec],
        out_specs=(full, full, pl.BlockSpec((block, latent), lambda i: (i, 0))),
        scratch_shapes=[pltpu.VMEM((nodes, latent), BF16)],
        compiler_params=pltpu.CompilerParams(vmem_limit_bytes=VMEM_LIMIT),
        name="mesh_encoder",
    )(src.reshape(edges // block, 1, block), a, b, c, mesh_feat, w_enc, w_send, w_recv, gain.reshape(1, latent))


def edge_kernel(dst_ref, rows_ref, q_ref, first_ref, w_edge, w_node, w_dec, gain, mesh_ref, dec_ref, sum_ref):
    i = pl.program_id(0)

    @pl.when(i == 0)
    def _():
        sum_ref[...] = jnp.zeros_like(sum_ref)

    block = rows_ref.shape[0]
    nodes = q_ref.shape[0]
    table = (lax.broadcasted_iota(jnp.int32, (nodes, block), 0) == dst_ref[0]).astype(BF16)
    near = lax.dot_general(table, q_ref[...], (((0,), (0,)), ((), ())), preferred_element_type=F32)
    joined = silu(rows_ref[...].astype(F32) + near).astype(BF16)
    sum_ref[...] += jnp.dot(table, joined, preferred_element_type=F32)

    @pl.when(i == pl.num_programs(0) - 1)
    def _():
        pooled = jnp.dot(sum_ref[...].astype(BF16), w_edge[...], preferred_element_type=F32)
        update = silu(jnp.dot(pooled.astype(BF16), w_node[...], preferred_element_type=F32))
        out = (first_ref[...].astype(F32) + gain[...] * layer_norm(update)).astype(BF16)
        mesh_ref[...] = out
        dec_ref[...] = jnp.dot(out, w_dec[...], preferred_element_type=F32).astype(BF16)


def edge_stage(dst, rows, q, first, w_edge, w_node, w_dec, gain):
    nodes, latent = first.shape
    edges = rows.shape[0]
    block = 512
    full = pl.BlockSpec((nodes, latent), lambda i: (0, 0))
    weight = pl.BlockSpec((latent, latent), lambda i: (0, 0))
    vec = pl.BlockSpec((1, latent), lambda i: (0, 0))
    out = jax.ShapeDtypeStruct((nodes, latent), BF16)
    return pl.pallas_call(
        edge_kernel,
        grid=(edges // block,),
        out_shape=(out, out),
        in_specs=[
            pl.BlockSpec((1, 1, block), lambda i: (i, 0, 0)),
            pl.BlockSpec((block, latent), lambda i: (i, 0)),
            full, full, weight, weight, weight, vec,
        ],
        out_specs=(full, full),
        scratch_shapes=[pltpu.VMEM((nodes, latent), F32)],
        compiler_params=pltpu.CompilerParams(vmem_limit_bytes=VMEM_LIMIT),
        name="mesh_edges",
    )(dst.reshape(edges // block, 1, block), rows, q, first, w_edge, w_node, w_dec, gain.reshape(1, latent))


def table_kernel(slot_ref, wgt_ref, out_ref):
    rows, slots = out_ref.shape
    ids = lax.broadcasted_iota(jnp.int32, (rows, slots), 1)
    total = jnp.zeros((rows, slots), F32)
    for k in range(slot_ref.shape[1]):
        total += jnp.where(ids == slot_ref[:, k : k + 1], wgt_ref[:, k : k + 1], 0.0)
    out_ref[...] = total.astype(BF16)


def decoder_table(slot, weight, slots):
    rows, k = slot.shape
    block = 256
    return pl.pallas_call(
        table_kernel,
        grid=(rows // block,),
        out_shape=jax.ShapeDtypeStruct((rows, slots), BF16),
        in_specs=[pl.BlockSpec((block, k), lambda i: (i, 0))] * 2,
        out_specs=pl.BlockSpec((block, slots), lambda i: (i, 0)),
        compiler_params=pltpu.CompilerParams(vmem_limit_bytes=VMEM_LIMIT),
        cost_estimate=pl.CostEstimate(flops=9 * rows * slots, bytes_accessed=2 * rows * slots, transcendentals=0),
        name="decoder_table",
    )(slot, weight)


def grid_kernel(table_ref, a_ref, b_ref, c_ref, grid_ref, w_out, gain, out_ref):
    per = a_ref.shape[0]
    total = jnp.dot(table_ref[:, :per], a_ref[...], preferred_element_type=F32)
    total += jnp.dot(table_ref[:, per : 2 * per], b_ref[...], preferred_element_type=F32)
    total += jnp.dot(table_ref[:, 2 * per :], c_ref[...], preferred_element_type=F32)
    update = silu(jnp.dot(total.astype(BF16), w_out[...], preferred_element_type=F32))
    out_ref[...] = (grid_ref[...].astype(F32) + gain[...] * layer_norm(update)).astype(BF16)


def grid_stage(table, west, mid, east, grid_feat, w_out, gain):
    rows, latent = grid_feat.shape
    slots = table.shape[1]
    block = 256
    full = pl.BlockSpec((slots // 3, latent), lambda i: (0, 0))
    return pl.pallas_call(
        grid_kernel,
        grid=(rows // block,),
        out_shape=jax.ShapeDtypeStruct((rows, latent), BF16),
        in_specs=[
            pl.BlockSpec((block, slots), lambda i: (i, 0)),
            full, full, full,
            pl.BlockSpec((block, latent), lambda i: (i, 0)),
            pl.BlockSpec((latent, latent), lambda i: (0, 0)),
            pl.BlockSpec((1, latent), lambda i: (0, 0)),
        ],
        out_specs=pl.BlockSpec((block, latent), lambda i: (i, 0)),
        compiler_params=pltpu.CompilerParams(vmem_limit_bytes=VMEM_LIMIT),
        name="mesh_to_grid",
    )(table, west, mid, east, grid_feat, w_out, gain.reshape(1, latent))


def ring(block, axis, distance):
    size = lax.axis_size(axis)
    return lax.ppermute(block, axis, [(i, (i + distance) % size) for i in range(size)])


def on_device(
    grid_feat, mesh_feat, g2m_src, g2m_dst, g2m_weight, mesh_src, mesh_dst, mesh_count, m2g_src, m2g_weight,
    w_in, w_enc, w_send, w_recv, w_edge, w_node, w_dec, w_out, gain_enc, gain_node, gain_out,
):
    grid_rows, latent = grid_feat.shape
    nodes = mesh_feat.shape[0]
    parts = latent // LANES
    lon_count = lax.axis_size("lon")
    tiles = lax.axis_size("lat") * lon_count
    band = lax.axis_index("lat")
    sector = lax.axis_index("lon")
    tile = band * lon_count + sector

    def tile_slot(ids):
        owner = ids // nodes
        step_lat = owner // lon_count - band + 1
        step_lon = (owner % lon_count - sector + 1) % lon_count
        return (step_lon * 3 + step_lat) * nodes + ids % nodes

    src4 = (g2m_src - tile * grid_rows) * parts
    dst4 = tile_slot(g2m_dst) * parts
    west, own, east = scatter(src4, dst4, g2m_weight, grid_feat, w_in, 9 * nodes)
    from_west = ring(east, "lon", 1)
    from_east = ring(west, "lon", -1)
    column = own.astype(F32) + from_west.astype(F32) + from_east.astype(F32)
    below = column[:nodes].astype(BF16)
    above = column[2 * nodes :].astype(BF16)
    center = column[nodes : 2 * nodes]
    from_below = ring(above, "lat", 1)
    from_above = ring(below, "lat", -1)

    capacity = mesh_src.shape[2]
    live = lax.broadcasted_iota(jnp.int32, (tiles, capacity), 1) < mesh_count[0][:, None]
    targets = jnp.where(live, mesh_dst[0] % nodes, nodes)
    target_in = lax.all_to_all(targets, ("lat", "lon"), split_axis=0, concat_axis=0, tiled=True)

    first, q, rows = node_stage(
        mesh_src[0] - tile * nodes, center, from_below, from_above, mesh_feat, w_enc, w_send, w_recv, gain_enc
    )
    rows_in = lax.all_to_all(
        rows.reshape(tiles, capacity, latent), ("lat", "lon"), split_axis=0, concat_axis=0, tiled=True
    ).reshape(tiles * capacity, latent)
    table = decoder_table(tile_slot(m2g_src), m2g_weight, 9 * nodes)

    mesh_out, decoded = edge_stage(target_in, rows_in, q, first, w_edge, w_node, w_dec, gain_node)

    mid = jnp.concatenate([ring(decoded, "lat", 1), decoded, ring(decoded, "lat", -1)], axis=0)
    grid_out = grid_stage(table, ring(mid, "lon", 1), mid, ring(mid, "lon", -1), grid_feat, w_out, gain_out)
    return (grid_out, mesh_out)


def solution(mesh):
    tile = ("lat", "lon")
    rows, flat, cube = P(tile, None), P(tile), P(tile, None, None)
    return jax.shard_map(
        on_device,
        mesh=mesh,
        in_specs=(rows, rows, flat, flat, flat, cube, cube, rows, rows, rows) + (P(),) * 11,
        out_specs=(rows, rows),
        check_vma=False,
    )
```

```python
import functools

import jax
import jax.numpy as jnp
from jax import lax
from jax.experimental import pallas as pl
from jax.experimental.pallas import tpu as pltpu
from jax.sharding import PartitionSpec as P

BF16 = jnp.bfloat16
F32 = jnp.float32
LANES = 128
MARKS = 8
MIB = 1024 * 1024
VMEM = pltpu.VMEM
SMEM = pltpu.SMEM
HBM = pltpu.HBM


def silu(v):
    half = 0.5 * v
    return half + half * jnp.tanh(half)


def layer_norm(values):
    center = values - jnp.mean(values, axis=-1, keepdims=True)
    spread = jnp.mean(center * center, axis=-1, keepdims=True)
    return center * lax.rsqrt(spread + 1e-05)


def whole(space=VMEM):
    return pl.BlockSpec(memory_space=space)


NEAR_A, NEAR_B, FAR_A, FAR_B, NEAR, FAR, A, OWN, B = range(9)
BY_PLACE = (NEAR_A, NEAR, NEAR_B, A, OWN, B, FAR_A, FAR, FAR_B)


def around_index(owner, band, sector, lon_count):
    step_lat = lax.shift_right_logical(owner, lon_count.bit_length() - 1) - band
    step_lon = ((owner - sector + 1) & (lon_count - 1)) - 1
    lat_at = 1 + step_lat * (2 * (band & 1) - 1)
    lon_at = 1 + step_lon * (2 * (sector & 1) - 1)
    place = lon_at * 3 + lat_at
    index = jnp.zeros_like(place)
    for at, tile in enumerate(BY_PLACE):
        if tile:
            index = jnp.where(place == at, tile, index)
    return index


def scatter_kernel(where_ref, src_hbm, dst_hbm, wgt_hbm, grid_hbm, w_hbm, *refs, nodes, lon_count):
    outs = refs[:5]
    accs = refs[5:9]
    y_ref, grid_ref, w_ref, src_v, dst_v, src_s, dst_s, wgt_s, grid_sem, sem = refs[9:]
    rows, latent = grid_ref.shape
    parts = latent // LANES
    step = 256
    chunks = rows // step

    def grid_copy(i):
        part = pl.ds(pl.multiple_of(i * step, step), step)
        return pltpu.make_async_copy(grid_hbm.at[part], grid_ref.at[part], grid_sem.at[i])

    src_in = pltpu.make_async_copy(src_hbm, src_v, sem.at[0])
    dst_in = pltpu.make_async_copy(dst_hbm, dst_v, sem.at[1])
    wgt_in = pltpu.make_async_copy(wgt_hbm, wgt_s, sem.at[2])
    w_in = pltpu.make_async_copy(w_hbm, w_ref, sem.at[3])
    for copy in (src_in, dst_in, wgt_in, w_in):
        copy.start()
    for i in range(chunks):
        grid_copy(i).start()
    band, sector, tile = where_ref[0], where_ref[1], where_ref[2]
    src_in.wait()
    src_v[...] = (src_v[...] - tile * rows) * parts
    src_out = pltpu.make_async_copy(src_v, src_s, sem.at[4])
    src_out.start()
    dst_in.wait()
    dst = dst_v[...]
    shift = nodes.bit_length() - 1
    index = around_index(lax.shift_right_logical(dst, shift), band, sector, lon_count)
    dst_v[...] = (index * nodes + (dst & (nodes - 1))) * parts
    dst_out = pltpu.make_async_copy(dst_v, dst_s, sem.at[5])
    dst_out.start()
    w_in.wait()

    span = accs[0].shape[0] // chunks
    zero = jnp.zeros((span, LANES), F32)

    def project(i, carry):
        grid_copy(i).wait()
        base = pl.multiple_of(i * step, step)
        y = silu(jnp.dot(grid_ref[pl.ds(base, step), :], w_ref[...], preferred_element_type=F32))
        for j in range(parts):
            y_ref[pl.ds(base * parts + j, step, stride=parts), :] = y[:, j * LANES : (j + 1) * LANES]
        for acc in accs:
            acc[pl.ds(pl.multiple_of(i * span, span), span), :] = zero
        return carry

    lax.fori_loop(0, chunks, project, 0)
    wgt_in.wait()
    src_out.wait()
    dst_out.wait()

    count = len(accs)
    lines, width = src_s.shape

    def add_edges(i, carry):
        for u in range(0, width, count):
            places, sums = [], []
            for n, acc in enumerate(accs):
                s = pl.multiple_of(src_s[i, u + n], parts)
                d = pl.multiple_of(dst_s[i, u + n], parts)
                places.append(d)
                sums.append(acc[pl.ds(d, parts), :] + wgt_s[i, u + n] * y_ref[pl.ds(s, parts), :])
            for acc, d, total in zip(accs, places, sums):
                acc[pl.ds(d, parts), :] = total
        return carry

    lax.fori_loop(0, lines, add_edges, 0)

    start = 0
    for out in outs:
        per = out.shape[0]

        def emit(i, carry, start=start, out=out):
            base = pl.multiple_of(i * step, step)
            for j in range(parts):
                rows_j = pl.ds((start + base) * parts + j, step, stride=parts)
                total = (accs[0][rows_j, :] + accs[1][rows_j, :]) + (accs[2][rows_j, :] + accs[3][rows_j, :])
                out[pl.ds(base, step), j * LANES : (j + 1) * LANES] = total.astype(out.dtype)
            return carry

        lax.fori_loop(0, per // step, emit, 0)
        start += per


def scatter(where, src, dst, weight, grid_feat, w_in, nodes, lon_count):
    rows, latent = grid_feat.shape
    parts = latent // LANES
    slots = 9 * nodes
    lines = src.shape[0] // LANES
    outs = tuple(jax.ShapeDtypeStruct((n * nodes, latent), BF16) for n in (2, 2, 1, 1, 3))
    ints = pltpu.VMEM((lines, LANES), jnp.int32)
    return pl.pallas_call(
        functools.partial(scatter_kernel, nodes=nodes, lon_count=lon_count),
        out_shape=outs,
        in_specs=[whole(SMEM)] + [whole(HBM)] * 5,
        out_specs=(whole(),) * 5,
        scratch_shapes=[pltpu.VMEM((slots * parts, LANES), F32)] * 4
        + [
            pltpu.VMEM((rows * parts, LANES), F32),
            pltpu.VMEM((rows, latent), BF16),
            pltpu.VMEM(w_in.shape, BF16),
            ints,
            ints,
            pltpu.SMEM((lines, LANES), jnp.int32),
            pltpu.SMEM((lines, LANES), jnp.int32),
            pltpu.SMEM((lines, LANES), F32),
            pltpu.SemaphoreType.DMA((rows // 256,)),
            pltpu.SemaphoreType.DMA((6,)),
        ],
        compiler_params=pltpu.CompilerParams(vmem_limit_bytes=60 * MIB),
        name="grid_to_mesh",
    )(where, *(v.reshape(lines, LANES) for v in (src, dst, weight)), grid_feat, w_in)


def column_kernel(own_ref, near_ref, far_ref, a_ref, b_ref):
    nodes = a_ref.shape[0]
    for n, out in enumerate((a_ref, b_ref)):
        part = slice(n * nodes, (n + 1) * nodes)
        mine = own_ref[2 * n * nodes : (2 * n + 1) * nodes, :].astype(F32)
        out[...] = (mine + near_ref[part, :].astype(F32) + far_ref[part, :].astype(F32)).astype(BF16)


def column_sums(own, near, far):
    nodes, latent = own.shape[0] // 3, own.shape[1]
    out = jax.ShapeDtypeStruct((nodes, latent), BF16)
    return pl.pallas_call(
        column_kernel,
        out_shape=(out, out),
        in_specs=[whole()] * 3,
        out_specs=(whole(),) * 2,
        compiler_params=pltpu.CompilerParams(vmem_limit_bytes=8 * MIB),
        name="column_sums",
    )(own, near, far)


def node_kernel(src_ref, mark_ref, own_ref, a_ref, b_ref, near_ref, far_ref, mesh_ref, enc_hbm, send_hbm, recv_hbm, gain, first_ref, q_ref, rows_hbm, rows_ref, w_enc, w_send, w_recv, sem, w_sem):
    tiles, _, _ = rows_ref.shape
    capacity = (rows_ref.shape[1] - MARKS) * LANES // mesh_ref.shape[1]
    parts = mesh_ref.shape[1] // LANES
    loads = [
        pltpu.make_async_copy(hbm, ref, w_sem.at[n])
        for n, (hbm, ref) in enumerate(((enc_hbm, w_enc), (send_hbm, w_send), (recv_hbm, w_recv)))
    ]
    for load in loads:
        load.start()
    nodes = mesh_ref.shape[0]
    pooled = own_ref[nodes : 2 * nodes, :].astype(F32)
    for ref in (a_ref, b_ref, near_ref, far_ref):
        pooled += ref[...].astype(F32)
    loads[0].wait()
    update = silu(jnp.dot(pooled.astype(BF16), w_enc[...], preferred_element_type=F32))
    first = (mesh_ref[...].astype(F32) + gain[...] * layer_norm(update)).astype(BF16)
    first_ref[...] = first
    loads[1].wait()
    p = jnp.dot(first, w_send[...], preferred_element_type=F32).astype(BF16)
    blocks, _, block = src_ref.shape
    per = block // capacity
    ids = lax.broadcasted_iota(jnp.int32, (nodes, block), 0)
    copies = []
    for i in range(blocks):
        table = (ids == src_ref[i]).astype(BF16)
        part = pl.ds(i * per, per)
        rows = lax.dot_general(table, p, (((0,), (0,)), ((), ())), preferred_element_type=F32).astype(BF16)
        for j in range(parts):
            rows_ref[part, j * capacity : (j + 1) * capacity, :] = rows[:, j * LANES : (j + 1) * LANES].reshape(
                per, capacity, LANES
            )
        mark = mark_ref[i * per : (i + 1) * per, :]
        rows_ref[part, parts * capacity :, :] = jnp.broadcast_to(mark[:, None, :], (per, MARKS, LANES)).astype(BF16)
        copies.append(pltpu.make_async_copy(rows_ref.at[part], rows_hbm.at[part], sem.at[i]))
        copies[-1].start()
    loads[2].wait()
    q_ref[...] = jnp.dot(first, w_recv[...], preferred_element_type=F32).astype(BF16)
    for copy in copies:
        copy.wait()


def node_stage(src, marks, sums, mesh_feat, w_enc, w_send, w_recv, gain):
    nodes, latent = mesh_feat.shape
    tiles, capacity = src.shape
    block = 512
    steps = tiles * capacity // block
    out = jax.ShapeDtypeStruct((nodes, latent), BF16)
    sent = (tiles, capacity * latent // LANES + MARKS, LANES)
    return pl.pallas_call(
        node_kernel,
        out_shape=(out, out, jax.ShapeDtypeStruct(sent, BF16)),
        in_specs=[whole()] * 8 + [whole(HBM)] * 3 + [whole()],
        out_specs=(whole(), whole(), whole(HBM)),
        scratch_shapes=[pltpu.VMEM(sent, BF16)]
        + [pltpu.VMEM((latent, latent), BF16)] * 3
        + [pltpu.SemaphoreType.DMA((steps,)), pltpu.SemaphoreType.DMA((3,))],
        compiler_params=pltpu.CompilerParams(vmem_limit_bytes=60 * MIB),
        name="mesh_encoder",
    )(src.reshape(steps, 1, block), marks, *sums, mesh_feat, w_enc, w_send, w_recv, gain.reshape(1, latent))


def edge_kernel(rows_ref, q_ref, first_ref, w_sum, w_dec, gain, mesh_ref, dec_ref, sum_ref):
    i = pl.program_id(0)
    tiles, height, _ = rows_ref.shape
    nodes, latent = q_ref.shape
    parts = latent // LANES
    capacity = (height - MARKS) // parts
    side = LANES // capacity
    per = 2 * side
    lane = lax.broadcasted_iota(jnp.int32, (MARKS, LANES), 1)
    ids = lax.broadcasted_iota(jnp.int32, (nodes // MARKS, MARKS, LANES), 0) * MARKS
    ids = (ids + lax.broadcasted_iota(jnp.int32, ids.shape, 1)).astype(F32)
    total = jnp.zeros(sum_ref.shape, F32)
    for b in range(tiles // per):
        halves = []
        for h in range(2):
            at = b * per + h * side
            mark = rows_ref[at, parts * capacity :, :].astype(F32)
            for k in range(1, side):
                mark = jnp.where(lane < k * capacity, mark, rows_ref[at + k, parts * capacity :, :].astype(F32))
            halves.append((ids == mark[None]).astype(BF16).reshape(nodes, LANES))
        table = jnp.concatenate(halves, axis=1)
        near = lax.dot_general(table, q_ref[...], (((0,), (0,)), ((), ())), preferred_element_type=F32)
        joined = []
        for j in range(parts):
            rows = rows_ref[b * per : (b + 1) * per, j * capacity : (j + 1) * capacity, :].reshape(per * capacity, LANES)
            joined.append(silu(rows.astype(F32) + near[:, j * LANES : (j + 1) * LANES]).astype(BF16))
        total += jnp.dot(table, jnp.concatenate(joined, axis=1), preferred_element_type=F32)

    @pl.when(i == 0)
    def _():
        sum_ref[...] = total

    @pl.when(i > 0)
    def _():
        sum_ref[...] += total

    @pl.when(i == pl.num_programs(0) - 1)
    def _():
        update = silu(jnp.dot(sum_ref[...].astype(BF16), w_sum[...], preferred_element_type=F32))
        out = (first_ref[...].astype(F32) + gain[...] * layer_norm(update)).astype(BF16)
        mesh_ref[...] = out
        dec_ref[...] = jnp.dot(out, w_dec[...], preferred_element_type=F32).astype(BF16)


def edge_stage(rows, q, first, w_sum, w_dec, gain):
    nodes, latent = first.shape
    tiles, height, _ = rows.shape
    block = 32
    full = pl.BlockSpec((nodes, latent), lambda i: (0, 0))
    weight = pl.BlockSpec((latent, latent), lambda i: (0, 0))
    vec = pl.BlockSpec((1, latent), lambda i: (0, 0))
    out = jax.ShapeDtypeStruct((nodes, latent), BF16)
    return pl.pallas_call(
        edge_kernel,
        grid=(tiles // block,),
        out_shape=(out, out),
        in_specs=[pl.BlockSpec((block, height, LANES), lambda i: (i, 0, 0)), full, full, weight, weight, vec],
        out_specs=(full, full),
        scratch_shapes=[pltpu.VMEM((nodes, latent), F32)],
        compiler_params=pltpu.CompilerParams(vmem_limit_bytes=14 * MIB),
        name="mesh_edges",
    )(rows, q, first, w_sum, w_dec, gain.reshape(1, latent))


def pick_table(picks, first_tile, tiles, nodes):
    rows, count = picks.shape[0], picks.shape[1] // 2
    ids = lax.broadcasted_iota(jnp.int32, (rows, LANES), 1).astype(jnp.int16)
    slots = [jnp.broadcast_to(picks[:, k : k + 1], (rows, LANES)).astype(jnp.int32).astype(jnp.int16) for k in range(count)]
    weights = [jnp.broadcast_to(picks[:, count + k : count + k + 1], (rows, LANES)).astype(BF16) for k in range(count)]
    blocks = []
    for j in range(first_tile * nodes // LANES, (first_tile + tiles) * nodes // LANES):
        at = ids + jnp.int16(j * LANES)
        block = jnp.zeros((rows, LANES), BF16)
        for slot, weight in zip(slots, weights):
            block = jnp.where(slot == at, weight, block)
        blocks.append(block)
    return jnp.concatenate(blocks, axis=1)


def first_kernel(picks_ref, near_ref, far_ref, a_ref, own_ref, b_ref, out_ref, *, inner):
    nodes = own_ref.shape[0]
    for i in range(out_ref.shape[0] // inner):
        part = slice(i * inner, (i + 1) * inner)
        table = pick_table(picks_ref[part, :], NEAR, 5, nodes)
        total = jnp.zeros((inner, out_ref.shape[1]), F32)
        for k, ref in enumerate((near_ref, far_ref, a_ref, own_ref, b_ref)):
            total += jnp.dot(table[:, k * nodes : (k + 1) * nodes], ref[...], preferred_element_type=F32)
        out_ref[part, :] = total.astype(BF16)


def first_stage(picks, near, far, a, own, b):
    rows = picks.shape[0]
    nodes, latent = own.shape
    block = 1024
    full = pl.BlockSpec((nodes, latent), lambda i: (0, 0))
    return pl.pallas_call(
        functools.partial(first_kernel, inner=256),
        grid=(rows // block,),
        out_shape=jax.ShapeDtypeStruct((rows, latent), BF16),
        in_specs=[pl.BlockSpec((block, picks.shape[1]), lambda i: (i, 0))] + [full] * 5,
        out_specs=pl.BlockSpec((block, latent), lambda i: (i, 0)),
        compiler_params=pltpu.CompilerParams(vmem_limit_bytes=16 * MIB),
        cost_estimate=pl.CostEstimate(flops=10 * rows * nodes * latent, bytes_accessed=8 * rows * latent, transcendentals=0),
        name="mesh_to_grid_first",
    )(picks, near, far, a, own, b)


def grid_kernel(picks_ref, part_ref, near_ref, far_ref, grid_ref, gain, out_ref, *, inner):
    nodes = near_ref.shape[0] // 2
    for i in range(out_ref.shape[0] // inner):
        part = slice(i * inner, (i + 1) * inner)
        table = pick_table(picks_ref[part, :], NEAR_A, 4, nodes)
        total = part_ref[part, :].astype(F32)
        total += jnp.dot(table[:, : 2 * nodes], near_ref[...], preferred_element_type=F32)
        total += jnp.dot(table[:, 2 * nodes :], far_ref[...], preferred_element_type=F32)
        update = silu(total)
        out_ref[part, :] = (grid_ref[part, :].astype(F32) + gain[...] * layer_norm(update)).astype(BF16)


def grid_stage(picks, part, near, far, grid_feat, gain):
    rows, latent = grid_feat.shape
    block = 512
    full = pl.BlockSpec(near.shape, lambda i: (0, 0))
    wide = pl.BlockSpec((block, latent), lambda i: (i, 0))
    return pl.pallas_call(
        functools.partial(grid_kernel, inner=256),
        grid=(rows // block,),
        out_shape=jax.ShapeDtypeStruct((rows, latent), BF16),
        in_specs=[
            pl.BlockSpec((block, picks.shape[1]), lambda i: (i, 0)),
            wide, full, full, wide,
            pl.BlockSpec((1, latent), lambda i: (0, 0)),
        ],
        out_specs=wide,
        compiler_params=pltpu.CompilerParams(vmem_limit_bytes=16 * MIB),
        name="mesh_to_grid",
    )(picks, part, near, far, grid_feat, gain.reshape(1, latent))


def swap(block, axis, first):
    size = lax.axis_size(axis)
    pairs = [(i, (i + 1 if (i % 2 == 0) == first else i - 1) % size) for i in range(size)]
    return lax.ppermute(block, axis, pairs)


def on_device(
    grid_feat, mesh_feat, g2m_src, g2m_dst, g2m_weight, mesh_src, mesh_dst, mesh_count, m2g_src, m2g_weight,
    w_in, w_enc, w_send, w_recv, w_edge, w_node, w_dec, w_out, gain_enc, gain_node, gain_out,
):
    grid_rows, latent = grid_feat.shape
    nodes = mesh_feat.shape[0]
    lon_count = lax.axis_size("lon")
    tiles = lax.axis_size("lat") * lon_count
    band = lax.axis_index("lat")
    sector = lax.axis_index("lon")
    tile = band * lon_count + sector
    where = jnp.stack([band, sector, tile]).astype(jnp.int32)

    near_ab, far_ab, near, far, own = scatter(where, g2m_src, g2m_dst, g2m_weight, grid_feat, w_in, nodes, lon_count)
    from_far_ab = swap(far_ab, "lon", False)
    from_near_ab = swap(near_ab, "lon", True)
    from_far = swap(far, "lon", False)
    from_near = swap(near, "lon", True)

    capacity = mesh_src.shape[2]
    live = lax.broadcasted_iota(jnp.int32, (tiles, capacity), 1) < mesh_count[0][:, None]
    marks = jnp.where(live, mesh_dst[0] & (nodes - 1), nodes).astype(F32)
    marks = jnp.tile(marks, (1, LANES // capacity))

    to_a, to_b = column_sums(own, from_near_ab, from_far_ab)
    sums = (own, swap(to_a, "lat", True), swap(to_b, "lat", False), from_near, from_far)

    first, q, rows = node_stage(
        mesh_src[0] - tile * nodes, marks, sums, mesh_feat, w_enc, w_send, w_recv, gain_enc
    )
    rows_in = lax.all_to_all(rows, ("lat", "lon"), split_axis=0, concat_axis=0, tiled=True)

    m2g_src, m2g_weight, first, w_edge, w_dec = lax.optimization_barrier((m2g_src, m2g_weight, first, w_edge, w_dec))
    shift = nodes.bit_length() - 1
    index = around_index(lax.shift_right_logical(m2g_src, shift), band, sector, lon_count)
    slots = index * nodes + (m2g_src & (nodes - 1))
    columns, weights = [slots[:, k] for k in range(slots.shape[1])], [m2g_weight[:, k] for k in range(slots.shape[1])]
    for i in range(len(columns)):
        for j in range(i + 1, len(columns)):
            same = columns[i] == columns[j]
            weights[i] = weights[i] + jnp.where(same, weights[j], 0.0)
            columns[j] = jnp.where(same, -1 - j, columns[j])
    picks = jnp.stack([c.astype(F32) for c in columns] + weights, axis=1)
    edge_node = jnp.dot(w_edge, w_node, preferred_element_type=F32).astype(BF16)
    dec_out = jnp.dot(w_dec, w_out, preferred_element_type=F32).astype(BF16)
    rows_in, picks, edge_node, dec_out = lax.optimization_barrier((rows_in, picks, edge_node, dec_out))

    mesh_out, decoded = edge_stage(rows_in, q, first, edge_node, dec_out, gain_node)

    from_a, from_b = swap(decoded, "lat", True), swap(decoded, "lat", False)
    far, near = swap(decoded, "lon", False), swap(decoded, "lon", True)
    ab = jnp.concatenate([from_a, from_b], axis=0)
    ab, near, far = lax.optimization_barrier((ab, near, far))
    far_ab, near_ab = swap(ab, "lon", False), swap(ab, "lon", True)
    part = first_stage(picks, near, far, from_a, decoded, from_b)
    grid_out = grid_stage(picks, part, near_ab, far_ab, grid_feat, gain_out)
    return (grid_out, mesh_out)


def solution(mesh):
    tile = ("lat", "lon")
    rows, flat, cube = P(tile, None), P(tile), P(tile, None, None)
    return jax.shard_map(
        on_device,
        mesh=mesh,
        in_specs=(rows, rows, flat, flat, flat, cube, cube, rows, rows, rows) + (P(),) * 11,
        out_specs=(rows, rows),
        check_vma=False,
    )
```

```python
import functools

import jax
import jax.numpy as jnp
from jax import lax
from jax.experimental import pallas as pl
from jax.experimental.pallas import tpu as pltpu
from jax.sharding import PartitionSpec as P

BF16 = jnp.bfloat16
F32 = jnp.float32
LANES = 128
MARKS = 8
MIB = 1024 * 1024
EDGE_MIB = 24
NODE_MIB = 57
VMEM = pltpu.VMEM
SMEM = pltpu.SMEM
HBM = pltpu.HBM


def silu(v):
    half = v * jnp.asarray(0.5, v.dtype)
    return half + half * jnp.tanh(half)


def layer_norm(values):
    center = values - jnp.mean(values, axis=-1, keepdims=True)
    spread = jnp.mean(center * center, axis=-1, keepdims=True)
    return center * lax.rsqrt(spread + 1e-05)


def whole(space=VMEM):
    return pl.BlockSpec(memory_space=space)


NEAR_A, NEAR_B, NEAR, FAR_A, FAR_B, FAR, A, B, OWN = range(9)
BY_PLACE = (NEAR_A, NEAR, NEAR_B, A, OWN, B, FAR_A, FAR, FAR_B)


def around_index(owner, band, sector, lon_count):
    step_lat = lax.shift_right_logical(owner, lon_count.bit_length() - 1) - band
    step_lon = ((owner - sector + 1) & (lon_count - 1)) - 1
    lat_at = 1 + step_lat * (2 * (band & 1) - 1)
    lon_at = 1 + step_lon * (2 * (sector & 1) - 1)
    place = lon_at * 3 + lat_at
    index = jnp.zeros_like(place)
    for at, tile in enumerate(BY_PLACE):
        if tile:
            index = jnp.where(place == at, tile, index)
    return index


def scatter_kernel(src_hbm, dst_hbm, wgt_hbm, grid_hbm, w_hbm, *refs, nodes, lon_count):
    count = len(refs) - 16
    outs = refs[:count]
    accs = refs[count : count + 4]
    y_ref, stage_ref, grid_ref, w_ref, src_v, dst_v, src_s, dst_s, wgt_s, grid_sem, out_sem, sem = refs[count + 4 :]
    rows, latent = grid_ref.shape
    parts = latent // LANES
    step = 256
    chunks = rows // step

    def grid_copy(i):
        part = pl.ds(pl.multiple_of(i * step, step), step)
        return pltpu.make_async_copy(grid_hbm.at[part], grid_ref.at[part], grid_sem.at[i])

    w_in = pltpu.make_async_copy(w_hbm, w_ref, sem.at[3])
    src_in = pltpu.make_async_copy(src_hbm, src_v, sem.at[0])
    dst_in = pltpu.make_async_copy(dst_hbm, dst_v, sem.at[1])
    wgt_in = pltpu.make_async_copy(wgt_hbm, wgt_s, sem.at[2])
    src_out = pltpu.make_async_copy(src_v, src_s, sem.at[4])
    dst_out = pltpu.make_async_copy(dst_v, dst_s, sem.at[5])
    w_in.start()
    grid_copy(0).start()
    for copy in (src_in, dst_in, wgt_in):
        copy.start()
    for i in range(1, chunks):
        grid_copy(i).start()
    w_in.wait()

    span = accs[0].shape[0] // chunks
    zero = jnp.zeros((span, LANES), F32)

    def project(i, carry):
        grid_copy(i).wait()
        base = pl.multiple_of(i * step, step)
        y = silu(jnp.dot(grid_ref[pl.ds(base, step), :], w_ref[...], preferred_element_type=F32))
        for j in range(parts):
            y_ref[pl.ds(base * parts + j, step, stride=parts), :] = y[:, j * LANES : (j + 1) * LANES]
        for acc in accs:
            acc[pl.ds(pl.multiple_of(i * span, span), span), :] = zero
        return carry

    project(0, 0)
    band, sector = lax.axis_index("lat"), lax.axis_index("lon")
    src_in.wait()
    src_v[...] = (src_v[...] - (band * lon_count + sector) * rows) * parts
    src_out.start()
    dst_in.wait()
    dst = dst_v[...]
    index = around_index(lax.shift_right_logical(dst, nodes.bit_length() - 1), band, sector, lon_count)
    dst_v[...] = (index * nodes + (dst & (nodes - 1))) * parts
    dst_out.start()
    lax.fori_loop(1, chunks, project, 0)
    wgt_in.wait()
    src_out.wait()
    dst_out.wait()

    count = len(accs)
    lines, width = src_s.shape

    def add_edges(i, carry):
        for u in range(0, width, count):
            places, sums = [], []
            for n, acc in enumerate(accs):
                s = pl.multiple_of(src_s[i, u + n], parts)
                d = pl.multiple_of(dst_s[i, u + n], parts)
                places.append(d)
                sums.append(acc[pl.ds(d, parts), :] + wgt_s[i, u + n] * y_ref[pl.ds(s, parts), :])
            for acc, d, total in zip(accs, places, sums):
                acc[pl.ds(d, parts), :] = total
        return carry

    lax.fori_loop(0, lines, add_edges, 0)

    def emit(i, carry):
        base = pl.multiple_of(i * step, step)
        for j in range(parts):
            rows_j = pl.ds(base * parts + j, step, stride=parts)
            total = (accs[0][rows_j, :] + accs[1][rows_j, :]) + (accs[2][rows_j, :] + accs[3][rows_j, :])
            stage_ref[pl.ds(base, step), j * LANES : (j + 1) * LANES] = total.astype(stage_ref.dtype)
        return carry

    copies, start = [], 0
    for n, out in enumerate(outs):
        per = out.shape[0]
        lax.fori_loop(start // step, (start + per) // step, emit, 0)
        copies.append(pltpu.make_async_copy(stage_ref.at[start : start + per], out, out_sem.at[n]))
        copies[-1].start()
        start += per
    for copy in copies:
        copy.wait()


def scatter(src, dst, weight, grid_feat, w_in, nodes, lon_count):
    rows, latent = grid_feat.shape
    parts = latent // LANES
    slots = 9 * nodes
    lines = src.shape[0] // LANES
    outs = tuple(jax.ShapeDtypeStruct((n * nodes, latent), BF16) for n in (2, 1, 2, 1, 2, 1))
    ints = pltpu.VMEM((lines, LANES), jnp.int32)
    return pl.pallas_call(
        functools.partial(scatter_kernel, nodes=nodes, lon_count=lon_count),
        out_shape=outs,
        in_specs=[whole(HBM)] * 5,
        out_specs=(whole(HBM),) * len(outs),
        scratch_shapes=[pltpu.VMEM((slots * parts, LANES), F32)] * 4
        + [
            pltpu.VMEM((rows * parts, LANES), F32),
            pltpu.VMEM((slots, latent), BF16),
            pltpu.VMEM((rows, latent), BF16),
            pltpu.VMEM(w_in.shape, BF16),
            ints,
            ints,
            pltpu.SMEM((lines, LANES), jnp.int32),
            pltpu.SMEM((lines, LANES), jnp.int32),
            pltpu.SMEM((lines, LANES), F32),
            pltpu.SemaphoreType.DMA((rows // 256,)),
            pltpu.SemaphoreType.DMA((6,)),
            pltpu.SemaphoreType.DMA((6,)),
        ],
        compiler_params=pltpu.CompilerParams(vmem_limit_bytes=60 * MIB),
        name="grid_to_mesh",
    )(*(v.reshape(lines, LANES) for v in (src, dst, weight)), grid_feat, w_in)


def add_kernel(a_ref, b_ref, *outs):
    rows = outs[0].shape[0]
    for n, out in enumerate(outs):
        part = slice(n * rows, (n + 1) * rows)
        out[...] = (a_ref[part, :].astype(F32) + b_ref[part, :].astype(F32)).astype(out.dtype)


def add_pieces(a, b, pieces, dtype, name):
    out = jax.ShapeDtypeStruct((a.shape[0] // pieces, a.shape[1]), dtype)
    return pl.pallas_call(
        add_kernel,
        out_shape=(out,) * pieces,
        in_specs=[whole()] * 2,
        out_specs=(whole(),) * pieces,
        compiler_params=pltpu.CompilerParams(vmem_limit_bytes=8 * MIB),
        name=name,
    )(a, b)


def node_kernel(src_ref, mark_ref, own_ref, a_ref, b_ref, near_ref, far_ref, mesh_ref, enc_hbm, send_hbm, recv_hbm, gain, first_ref, q_ref, rows_hbm, rows_ref, w_enc, w_send, w_recv, sem, w_sem):
    tiles, _, _ = rows_ref.shape
    capacity = (rows_ref.shape[1] - MARKS) * LANES // mesh_ref.shape[1]
    parts = mesh_ref.shape[1] // LANES
    loads = [
        pltpu.make_async_copy(hbm, ref, w_sem.at[n])
        for n, (hbm, ref) in enumerate(((enc_hbm, w_enc), (send_hbm, w_send), (recv_hbm, w_recv)))
    ]
    for load in loads:
        load.start()
    nodes = mesh_ref.shape[0]
    pooled = own_ref[...].astype(F32)
    for ref in (a_ref, b_ref, near_ref, far_ref):
        pooled += ref[ref.shape[0] - nodes :, :].astype(F32)
    loads[0].wait()
    update = silu(jnp.dot(pooled.astype(BF16), w_enc[...], preferred_element_type=F32))
    first = (mesh_ref[...].astype(F32) + gain[...] * layer_norm(update)).astype(BF16)
    first_ref[...] = first
    loads[1].wait()
    p = jnp.dot(first, w_send[...], preferred_element_type=F32).astype(BF16)
    blocks, _, block = src_ref.shape
    per = block // capacity
    ids = lax.broadcasted_iota(jnp.int32, (nodes, block), 0)
    copies = []
    for i in range(blocks):
        table = (ids == src_ref[i]).astype(BF16)
        part = pl.ds(i * per, per)
        rows = lax.dot_general(table, p, (((0,), (0,)), ((), ())), preferred_element_type=F32).astype(BF16)
        for j in range(parts):
            rows_ref[part, j * capacity : (j + 1) * capacity, :] = rows[:, j * LANES : (j + 1) * LANES].reshape(
                per, capacity, LANES
            )
        mark = mark_ref[i * per : (i + 1) * per, :]
        rows_ref[part, parts * capacity :, :] = jnp.broadcast_to(mark[:, None, :], (per, MARKS, LANES)).astype(BF16)
        copies.append(pltpu.make_async_copy(rows_ref.at[part], rows_hbm.at[part], sem.at[i]))
        copies[-1].start()
    loads[2].wait()
    q_ref[...] = jnp.dot(first, w_recv[...], preferred_element_type=F32).astype(BF16)
    for copy in copies:
        copy.wait()


def node_stage(src, marks, sums, mesh_feat, w_enc, w_send, w_recv, gain):
    nodes, latent = mesh_feat.shape
    tiles, capacity = src.shape
    block = 512
    steps = tiles * capacity // block
    out = jax.ShapeDtypeStruct((nodes, latent), BF16)
    sent = (tiles, capacity * latent // LANES + MARKS, LANES)
    return pl.pallas_call(
        node_kernel,
        out_shape=(out, out, jax.ShapeDtypeStruct(sent, BF16)),
        in_specs=[whole()] * 8 + [whole(HBM)] * 3 + [whole()],
        out_specs=(whole(), whole(), whole(HBM)),
        scratch_shapes=[pltpu.VMEM(sent, BF16)]
        + [pltpu.VMEM((latent, latent), BF16)] * 3
        + [pltpu.SemaphoreType.DMA((steps,)), pltpu.SemaphoreType.DMA((3,))],
        compiler_params=pltpu.CompilerParams(vmem_limit_bytes=NODE_MIB * MIB),
        name="mesh_encoder",
    )(src.reshape(steps, 1, block), marks, *sums, mesh_feat, w_enc, w_send, w_recv, gain.reshape(1, latent))


def edge_kernel(rows_hbm, q_ref, first_ref, w_sum, w_dec, gain, mesh_ref, dec_ref, rows_ref, sem, *, per):
    tiles, height, _ = rows_ref.shape
    nodes, latent = q_ref.shape
    parts = latent // LANES
    capacity = (height - MARKS) // parts
    side = LANES // capacity
    steps = tiles // per
    loads = []
    for b in range(steps):
        part = pl.ds(b * per, per)
        loads.append(pltpu.make_async_copy(rows_hbm.at[part], rows_ref.at[part], sem.at[b]))
        loads[-1].start()
    lane = lax.broadcasted_iota(jnp.int32, (MARKS, LANES), 1)
    ids = lax.broadcasted_iota(jnp.int32, (nodes // 16, 16, LANES), 0) * 16
    ids = (ids + lax.broadcasted_iota(jnp.int32, ids.shape, 1)).astype(F32).astype(BF16)
    one, zero = jnp.ones((), BF16), jnp.zeros((), BF16)
    total = jnp.zeros((nodes, latent), F32)
    for b in range(steps):
        loads[b].wait()
        pieces = []
        for at in range(b * per, (b + 1) * per, side):
            mark = rows_ref[at, parts * capacity :, :].astype(F32)
            for k in range(1, side):
                mark = jnp.where(lane < k * capacity, mark, rows_ref[at + k, parts * capacity :, :].astype(F32))
            mark = jnp.concatenate([mark] * (16 // MARKS), axis=0).astype(BF16)
            pieces.append(jnp.where(ids == mark[None], one, zero).reshape(nodes, LANES))
        table = jnp.concatenate(pieces, axis=1)
        near = lax.dot_general(table, q_ref[...], (((0,), (0,)), ((), ())), preferred_element_type=F32)
        joined = []
        for j in range(parts):
            rows = rows_ref[b * per : (b + 1) * per, j * capacity : (j + 1) * capacity, :].reshape(per * capacity, LANES)
            joined.append(silu((rows.astype(F32) + near[:, j * LANES : (j + 1) * LANES]).astype(BF16)))
        total += jnp.dot(table, jnp.concatenate(joined, axis=1), preferred_element_type=F32)
    update = silu(jnp.dot(total.astype(BF16), w_sum[...], preferred_element_type=F32))
    out = (first_ref[...].astype(F32) + gain[...] * layer_norm(update)).astype(BF16)
    mesh_ref[...] = out
    dec_ref[...] = jnp.dot(out, w_dec[...], preferred_element_type=F32).astype(BF16)


def edge_stage(rows, q, first, w_sum, w_dec, gain):
    nodes, latent = first.shape
    per = 16
    out = jax.ShapeDtypeStruct((nodes, latent), BF16)
    return pl.pallas_call(
        functools.partial(edge_kernel, per=per),
        out_shape=(out, out),
        in_specs=[whole(HBM)] + [whole()] * 5,
        out_specs=(whole(), whole()),
        scratch_shapes=[pltpu.VMEM(rows.shape, BF16), pltpu.SemaphoreType.DMA((rows.shape[0] // per,))],
        compiler_params=pltpu.CompilerParams(vmem_limit_bytes=EDGE_MIB * MIB),
        name="mesh_edges",
    )(rows, q, first, w_sum, w_dec, gain.reshape(1, latent))


def pick_table(picks, tiles, nodes):
    rows, count = picks.shape[0], picks.shape[1] // 2
    ids = lax.broadcasted_iota(jnp.int32, (rows, LANES), 1).astype(jnp.int16)
    slots = [jnp.broadcast_to(picks[:, k : k + 1], (rows, LANES)).astype(jnp.int32).astype(jnp.int16) for k in range(count)]
    weights = [jnp.broadcast_to(picks[:, count + k : count + k + 1], (rows, LANES)).astype(BF16) for k in range(count)]
    blocks = []
    for j in (t * nodes // LANES + n for t in tiles for n in range(nodes // LANES)):
        at = ids + jnp.int16(j * LANES)
        block = jnp.zeros((rows, LANES), BF16)
        for slot, weight in zip(slots, weights):
            block = jnp.where(slot == at, weight, block)
        blocks.append(block)
    return jnp.concatenate(blocks, axis=1)


def first_kernel(picks_ref, tiles_ref, out_ref, *, tiles, inner):
    nodes = tiles_ref.shape[0] // len(tiles)
    for i in range(out_ref.shape[0] // inner):
        part = slice(i * inner, (i + 1) * inner)
        table = pick_table(picks_ref[part, :], tiles, nodes)
        out_ref[part, :] = jnp.dot(table, tiles_ref[...], preferred_element_type=F32).astype(BF16)


def first_stage(picks, tiles, source):
    rows, latent = picks.shape[0], source.shape[1]
    block = 512
    wide = pl.BlockSpec((block, latent), lambda i: (i, 0))
    return pl.pallas_call(
        functools.partial(first_kernel, tiles=tiles, inner=256),
        grid=(rows // block,),
        out_shape=jax.ShapeDtypeStruct((rows, latent), BF16),
        in_specs=[pl.BlockSpec((block, picks.shape[1]), lambda i: (i, 0)), pl.BlockSpec(source.shape, lambda i: (0, 0))],
        out_specs=wide,
        compiler_params=pltpu.CompilerParams(vmem_limit_bytes=16 * MIB),
        cost_estimate=pl.CostEstimate(
            flops=2 * rows * source.size, bytes_accessed=8 * rows * latent, transcendentals=0
        ),
        name="mesh_to_grid_first",
    )(picks, source)


def grid_kernel(picks_ref, part_ref, near_ref, far_ref, grid_ref, gain, out_ref, *, inner, tiles, nodes):
    width = near_ref.shape[0]
    for i in range(out_ref.shape[0] // inner):
        part = slice(i * inner, (i + 1) * inner)
        table = pick_table(picks_ref[part, :], tiles, nodes)
        total = part_ref[part, :].astype(F32)
        total += jnp.dot(table[:, :width], near_ref[...], preferred_element_type=F32)
        total += jnp.dot(table[:, width:], far_ref[...], preferred_element_type=F32)
        update = silu(total)
        out_ref[part, :] = (grid_ref[part, :].astype(F32) + gain[...] * layer_norm(update)).astype(BF16)


def grid_stage(picks, part, tiles, near, far, grid_feat, gain):
    rows, latent = grid_feat.shape
    block = 512
    full = pl.BlockSpec(near.shape, lambda i: (0, 0))
    wide = pl.BlockSpec((block, latent), lambda i: (i, 0))
    return pl.pallas_call(
        functools.partial(grid_kernel, inner=256, tiles=tiles, nodes=2 * near.shape[0] // len(tiles)),
        grid=(rows // block,),
        out_shape=jax.ShapeDtypeStruct((rows, latent), BF16),
        in_specs=[
            pl.BlockSpec((block, picks.shape[1]), lambda i: (i, 0)),
            wide, full, full, wide,
            pl.BlockSpec((1, latent), lambda i: (0, 0)),
        ],
        out_specs=wide,
        compiler_params=pltpu.CompilerParams(vmem_limit_bytes=16 * MIB),
        name="mesh_to_grid",
    )(picks, part, near, far, grid_feat, gain.reshape(1, latent))


def stack_kernel(near_ref, far_ref, a_ref, b_ref, own_ref, pair_ref, five_ref):
    nodes = own_ref.shape[0]
    for n, ref in enumerate((near_ref, far_ref, a_ref, b_ref, own_ref)):
        five_ref[n * nodes : (n + 1) * nodes, :] = ref[...]
    pair_ref[:nodes, :] = a_ref[...]
    pair_ref[nodes:, :] = b_ref[...]


def stack_tiles(near, far, a, b, own):
    nodes, latent = own.shape
    return pl.pallas_call(
        stack_kernel,
        out_shape=tuple(jax.ShapeDtypeStruct((n * nodes, latent), BF16) for n in (2, 5)),
        in_specs=[whole()] * 5,
        out_specs=(whole(),) * 2,
        compiler_params=pltpu.CompilerParams(vmem_limit_bytes=8 * MIB),
        name="stack_tiles",
    )(near, far, a, b, own)


def swap(block, axis, first):
    size = lax.axis_size(axis)
    pairs = [(i, (i + 1 if (i % 2 == 0) == first else i - 1) % size) for i in range(size)]
    return lax.ppermute(block, axis, pairs)


def on_device(
    grid_feat, mesh_feat, g2m_src, g2m_dst, g2m_weight, mesh_src, mesh_dst, mesh_count, m2g_src, m2g_weight,
    w_in, w_enc, w_send, w_recv, w_edge, w_node, w_dec, w_out, gain_enc, gain_node, gain_out,
):
    grid_rows, latent = grid_feat.shape
    nodes = mesh_feat.shape[0]
    lon_count = lax.axis_size("lon")
    tiles = lax.axis_size("lat") * lon_count
    band = lax.axis_index("lat")
    sector = lax.axis_index("lon")
    tile = band * lon_count + sector

    near_ab, near, far_ab, far, own_ab, own = scatter(g2m_src, g2m_dst, g2m_weight, grid_feat, w_in, nodes, lon_count)
    from_far_ab = swap(far_ab, "lon", False)
    from_near_ab = swap(near_ab, "lon", True)
    from_far = swap(far, "lon", False)
    from_near = swap(near, "lon", True)

    capacity = mesh_src.shape[2]
    live = lax.broadcasted_iota(jnp.int32, (tiles, capacity), 1) < mesh_count[0][:, None]
    marks = jnp.where(live, mesh_dst[0] & (nodes - 1), nodes).astype(F32)
    marks = jnp.tile(marks, (1, LANES // capacity))

    (own_ab,) = add_pieces(own_ab, from_near_ab, 1, F32, "add_near")
    to_a, to_b = add_pieces(own_ab, from_far_ab, 2, BF16, "add_far")
    sums = (own, swap(to_a, "lat", True), swap(to_b, "lat", False), from_near, from_far)

    first, q, rows = node_stage(
        mesh_src[0] - tile * nodes, marks, sums, mesh_feat, w_enc, w_send, w_recv, gain_enc
    )
    rows_in = lax.all_to_all(rows, ("lat", "lon"), split_axis=0, concat_axis=0, tiled=True)

    m2g_src, m2g_weight, first, w_edge, w_dec = lax.optimization_barrier((m2g_src, m2g_weight, first, w_edge, w_dec))
    shift = nodes.bit_length() - 1
    index = around_index(lax.shift_right_logical(m2g_src, shift), band, sector, lon_count)
    slots = index * nodes + (m2g_src & (nodes - 1))
    columns, weights = [slots[:, k] for k in range(slots.shape[1])], [m2g_weight[:, k] for k in range(slots.shape[1])]
    for i in range(len(columns)):
        for j in range(i + 1, len(columns)):
            same = columns[i] == columns[j]
            weights[i] = weights[i] + jnp.where(same, weights[j], 0.0)
            columns[j] = jnp.where(same, -1 - j, columns[j])
    picks = jnp.stack([c.astype(F32) for c in columns] + weights, axis=1)
    edge_node = jnp.dot(w_edge, w_node, preferred_element_type=F32).astype(BF16)
    dec_out = jnp.dot(w_dec, w_out, preferred_element_type=F32).astype(BF16)
    rows_in, picks, edge_node, dec_out = lax.optimization_barrier((rows_in, picks, edge_node, dec_out))

    mesh_out, decoded = edge_stage(rows_in, q, first, edge_node, dec_out, gain_node)

    from_a, from_b = swap(decoded, "lat", True), swap(decoded, "lat", False)
    far, near = swap(decoded, "lon", False), swap(decoded, "lon", True)
    pair, five = stack_tiles(near, far, from_a, from_b, decoded)
    far_pair, near_pair = swap(pair, "lon", False), swap(pair, "lon", True)
    part = first_stage(picks, (NEAR, FAR, A, B, OWN), five)
    late = (NEAR_A, NEAR_B, FAR_A, FAR_B)
    grid_out = grid_stage(picks, part, late, near_pair, far_pair, grid_feat, gain_out)
    return (grid_out, mesh_out)


def solution(mesh):
    tile = ("lat", "lon")
    rows, flat, cube = P(tile, None), P(tile), P(tile, None, None)
    return jax.shard_map(
        on_device,
        mesh=mesh,
        in_specs=(rows, rows, flat, flat, flat, cube, cube, rows, rows, rows) + (P(),) * 11,
        out_specs=(rows, rows),
        check_vma=False,
    )
```

```python
import functools

import jax
import jax.numpy as jnp
from jax import lax
from jax.experimental import pallas as pl
from jax.experimental.pallas import tpu as pltpu
from jax.sharding import PartitionSpec as P

BF16 = jnp.bfloat16
F32 = jnp.float32
LANES = 128
MARKS = 8
MIB = 1024 * 1024
EDGE_MIB = 24
NODE_MIB = 57
VMEM = pltpu.VMEM
SMEM = pltpu.SMEM
HBM = pltpu.HBM


def silu_of_half(half):
    return half + half * jnp.tanh(half)


def silu(v):
    half = v * jnp.asarray(0.5, v.dtype)
    return half + half * jnp.tanh(half)


def layer_norm(values):
    center = values - jnp.mean(values, axis=-1, keepdims=True)
    spread = jnp.mean(center * center, axis=-1, keepdims=True)
    return center * lax.rsqrt(spread + 1e-05)


def whole(space=VMEM):
    return pl.BlockSpec(memory_space=space)


NEAR_A, NEAR_B, NEAR, FAR_A, FAR_B, FAR, A, B, OWN = range(9)
BY_PLACE = (NEAR_A, NEAR, NEAR_B, A, OWN, B, FAR_A, FAR, FAR_B)


def around_index(owner, band, sector, lon_count):
    step_lat = lax.shift_right_logical(owner, lon_count.bit_length() - 1) - band
    step_lon = ((owner - sector + 1) & (lon_count - 1)) - 1
    lat_at = 1 + step_lat * (2 * (band & 1) - 1)
    lon_at = 1 + step_lon * (2 * (sector & 1) - 1)
    place = lon_at * 3 + lat_at
    index = jnp.zeros_like(place)
    for at, tile in enumerate(BY_PLACE):
        if tile:
            index = jnp.where(place == at, tile, index)
    return index


def scatter_kernel(src_hbm, dst_hbm, wgt_hbm, grid_hbm, w_hbm, *refs, nodes, lon_count):
    count = len(refs) - 17
    outs = refs[:count]
    accs = refs[count : count + 4]
    y_ref, stage_ref, grid_ref, w_ref, wide_ref, src_v, dst_v, wgt_v, src_s, dst_s, grid_sem, out_sem, sem = refs[count + 4 :]
    rows, latent = grid_ref.shape
    parts = latent // LANES
    step = 256
    chunks = rows // step

    def grid_copy(i):
        part = pl.ds(pl.multiple_of(i * step, step), step)
        return pltpu.make_async_copy(grid_hbm.at[part], grid_ref.at[part], grid_sem.at[i])

    w_in = pltpu.make_async_copy(w_hbm, w_ref, sem.at[3])
    src_in = pltpu.make_async_copy(src_hbm, src_v, sem.at[0])
    dst_in = pltpu.make_async_copy(dst_hbm, dst_v, sem.at[1])
    wgt_in = pltpu.make_async_copy(wgt_hbm, wgt_v, sem.at[2])
    src_out = pltpu.make_async_copy(src_v, src_s, sem.at[4])
    dst_out = pltpu.make_async_copy(dst_v, dst_s, sem.at[5])
    for copy in (wgt_in, w_in, grid_copy(0), src_in, dst_in):
        copy.start()
    for i in range(1, chunks):
        grid_copy(i).start()
    lines, width = src_s.shape
    wgt_in.wait()
    turned = jnp.transpose(wgt_v[...])
    for i in range(lines):
        wide_ref[i * width : (i + 1) * width, :] = jnp.broadcast_to(turned[:, i : i + 1], (width, LANES))
    w_in.wait()

    span = accs[0].shape[0] // chunks
    zero = jnp.zeros((span, LANES), F32)

    def project(i, carry):
        grid_copy(i).wait()
        base = pl.multiple_of(i * step, step)
        y = silu(jnp.dot(grid_ref[pl.ds(base, step), :], w_ref[...], preferred_element_type=F32))
        for j in range(parts):
            y_ref[pl.ds(base * parts + j, step, stride=parts), :] = y[:, j * LANES : (j + 1) * LANES]
        for acc in accs:
            acc[pl.ds(pl.multiple_of(i * span, span), span), :] = zero
        return carry

    project(0, 0)
    band, sector = lax.axis_index("lat"), lax.axis_index("lon")
    src_in.wait()
    src_v[...] = (src_v[...] - (band * lon_count + sector) * rows) * parts
    src_out.start()
    dst_in.wait()
    dst = dst_v[...]
    index = around_index(lax.shift_right_logical(dst, nodes.bit_length() - 1), band, sector, lon_count)
    dst_v[...] = (index * nodes + (dst & (nodes - 1))) * parts
    dst_out.start()
    lax.fori_loop(1, chunks, project, 0)
    src_out.wait()
    dst_out.wait()

    count = len(accs)

    def add_edges(i, carry):
        for u in range(0, width, count):
            places, sums = [], []
            for n, acc in enumerate(accs):
                s = pl.multiple_of(src_s[i, u + n], parts)
                d = pl.multiple_of(dst_s[i, u + n], parts)
                places.append(d)
                w = wide_ref[pl.ds(i * width + u + n, 1), :]
                sums.append(acc[pl.ds(d, parts), :] + w * y_ref[pl.ds(s, parts), :])
            for acc, d, total in zip(accs, places, sums):
                acc[pl.ds(d, parts), :] = total
        return carry

    lax.fori_loop(0, lines, add_edges, 0)

    def emit(i, carry):
        base = pl.multiple_of(i * step, step)
        for j in range(parts):
            rows_j = pl.ds(base * parts + j, step, stride=parts)
            total = (accs[0][rows_j, :] + accs[1][rows_j, :]) + (accs[2][rows_j, :] + accs[3][rows_j, :])
            stage_ref[pl.ds(base, step), j * LANES : (j + 1) * LANES] = total.astype(stage_ref.dtype)
        return carry

    copies, start = [], 0
    for n, out in enumerate(outs):
        per = out.shape[0]
        lax.fori_loop(start // step, (start + per) // step, emit, 0)
        copies.append(pltpu.make_async_copy(stage_ref.at[start : start + per], out, out_sem.at[n]))
        copies[-1].start()
        start += per
    for copy in copies:
        copy.wait()


def scatter(src, dst, weight, grid_feat, w_in, nodes, lon_count):
    rows, latent = grid_feat.shape
    parts = latent // LANES
    slots = 9 * nodes
    lines = src.shape[0] // LANES
    outs = tuple(jax.ShapeDtypeStruct((n * nodes, latent), BF16) for n in (2, 1, 1, 1, 1, 2, 1))
    ints = pltpu.VMEM((lines, LANES), jnp.int32)
    return pl.pallas_call(
        functools.partial(scatter_kernel, nodes=nodes, lon_count=lon_count),
        out_shape=outs,
        in_specs=[whole(HBM)] * 5,
        out_specs=(whole(HBM),) * len(outs),
        scratch_shapes=[pltpu.VMEM((slots * parts, LANES), F32)] * 4
        + [
            pltpu.VMEM((rows * parts, LANES), F32),
            pltpu.VMEM((slots, latent), BF16),
            pltpu.VMEM((rows, latent), BF16),
            pltpu.VMEM(w_in.shape, BF16),
            pltpu.VMEM((lines * LANES, LANES), F32),
            ints,
            ints,
            pltpu.VMEM((lines, LANES), F32),
            pltpu.SMEM((lines, LANES), jnp.int32),
            pltpu.SMEM((lines, LANES), jnp.int32),
            pltpu.SemaphoreType.DMA((rows // 256,)),
            pltpu.SemaphoreType.DMA((7,)),
            pltpu.SemaphoreType.DMA((6,)),
        ],
        compiler_params=pltpu.CompilerParams(vmem_limit_bytes=60 * MIB),
        name="grid_to_mesh",
    )(*(v.reshape(lines, LANES) for v in (src, dst, weight)), grid_feat, w_in)


def add_kernel(a_ref, b_ref, *outs):
    start = 0
    for out in outs:
        part = slice(start, start + out.shape[0])
        out[...] = (a_ref[part, :].astype(F32) + b_ref[part, :].astype(F32)).astype(out.dtype)
        start += out.shape[0]


def add_near(own, near):
    out = jax.ShapeDtypeStruct((own.shape[0] // 2, own.shape[1]), F32)
    return pl.pallas_call(
        add_kernel,
        out_shape=(out, out),
        in_specs=[whole()] * 2,
        out_specs=(whole(),) * 2,
        compiler_params=pltpu.CompilerParams(vmem_limit_bytes=8 * MIB),
        name="add_near",
    )(own, near)


def add_far(far, own):
    return pl.pallas_call(
        add_kernel,
        out_shape=jax.ShapeDtypeStruct(far.shape, BF16),
        in_specs=[whole()] * 2,
        out_specs=whole(),
        compiler_params=pltpu.CompilerParams(vmem_limit_bytes=8 * MIB),
        name="add_far",
    )(far, own)


def node_kernel(*refs, pieces):
    count = pieces + 7
    sources, (first_hbm, q_hbm, rows_hbm), held = refs[:count], refs[count : count + 3], refs[count + 3 : 2 * count + 3]
    first_ref, q_ref, rows_ref, in_sem, out_sem, sem = refs[2 * count + 3 :]
    loads = [pltpu.make_async_copy(a, b, in_sem.at[n]) for n, (a, b) in enumerate(zip(sources, held))]
    for load in loads:
        load.start()
    w_enc, mesh_ref, gain, w_send, w_recv, src_ref, mark_ref = held[pieces:]
    nodes, latent = mesh_ref.shape
    capacity = (rows_ref.shape[1] - MARKS) * LANES // latent
    parts = latent // LANES
    loads[0].wait()
    pooled = held[0][...].astype(F32)
    for n in range(1, pieces):
        loads[n].wait()
        pooled += held[n][...].astype(F32)
    loads[pieces].wait()
    update = silu(jnp.dot(pooled.astype(BF16), w_enc[...], preferred_element_type=F32))
    for load in loads[pieces + 1 :]:
        load.wait()
    first = (mesh_ref[...].astype(F32) + gain[...] * layer_norm(update)).astype(BF16)
    first_ref[...] = first
    first_out = pltpu.make_async_copy(first_ref, first_hbm, out_sem.at[0])
    first_out.start()
    p = (0.5 * jnp.dot(first, w_send[...], preferred_element_type=F32)).astype(BF16)
    blocks, _, block = src_ref.shape
    per = block // capacity
    ids = lax.broadcasted_iota(jnp.int32, (nodes, block), 0)
    copies = []
    for i in range(blocks):
        table = (ids == src_ref[i]).astype(BF16)
        part = pl.ds(i * per, per)
        rows = lax.dot_general(table, p, (((0,), (0,)), ((), ())), preferred_element_type=F32).astype(BF16)
        for j in range(parts):
            rows_ref[part, j * capacity : (j + 1) * capacity, :] = rows[:, j * LANES : (j + 1) * LANES].reshape(
                per, capacity, LANES
            )
        mark = mark_ref[i * per : (i + 1) * per, :]
        rows_ref[part, parts * capacity :, :] = jnp.broadcast_to(mark[:, None, :], (per, MARKS, LANES)).astype(BF16)
        copies.append(pltpu.make_async_copy(rows_ref.at[part], rows_hbm.at[part], sem.at[i]))
        copies[-1].start()
    q_ref[...] = (0.5 * jnp.dot(first, w_recv[...], preferred_element_type=F32)).astype(BF16)
    q_out = pltpu.make_async_copy(q_ref, q_hbm, out_sem.at[1])
    q_out.start()
    for copy in (first_out, q_out, *copies):
        copy.wait()


def node_stage(src, marks, sums, mesh_feat, w_enc, w_send, w_recv, gain):
    nodes, latent = mesh_feat.shape
    tiles, capacity = src.shape
    block = 512
    steps = tiles * capacity // block
    out = jax.ShapeDtypeStruct((nodes, latent), BF16)
    sent = (tiles, capacity * latent // LANES + MARKS, LANES)
    inputs = (*sums, w_enc, mesh_feat, gain.reshape(1, latent), w_send, w_recv, src.reshape(steps, 1, block), marks)
    return pl.pallas_call(
        functools.partial(node_kernel, pieces=len(sums)),
        out_shape=(out, out, jax.ShapeDtypeStruct(sent, BF16)),
        in_specs=[whole(HBM)] * len(inputs),
        out_specs=(whole(HBM),) * 3,
        scratch_shapes=[pltpu.VMEM(v.shape, v.dtype) for v in inputs]
        + [pltpu.VMEM((nodes, latent), BF16)] * 2
        + [pltpu.VMEM(sent, BF16)]
        + [pltpu.SemaphoreType.DMA((n,)) for n in (len(inputs), 2, steps)],
        compiler_params=pltpu.CompilerParams(vmem_limit_bytes=NODE_MIB * MIB),
        name="mesh_encoder",
    )(*inputs)


def edge_kernel(rows_hbm, q_ref, first_ref, w_sum, w_dec, gain, mesh_hbm, dec_ref, rows_ref, mesh_ref, sem, out_sem, *, per):
    tiles, height, _ = rows_ref.shape
    nodes, latent = q_ref.shape
    parts = latent // LANES
    capacity = (height - MARKS) // parts
    side = LANES // capacity
    steps = tiles // per
    loads = []
    for b in range(steps):
        part = pl.ds(b * per, per)
        loads.append(pltpu.make_async_copy(rows_hbm.at[part], rows_ref.at[part], sem.at[b]))
        loads[-1].start()
    lane = lax.broadcasted_iota(jnp.int32, (MARKS, LANES), 1)
    ids = lax.broadcasted_iota(jnp.int32, (nodes // 16, 16, LANES), 0) * 16
    ids = (ids + lax.broadcasted_iota(jnp.int32, ids.shape, 1)).astype(F32).astype(BF16)
    one, zero = jnp.ones((), BF16), jnp.zeros((), BF16)
    total = jnp.zeros((nodes, latent), F32)
    for b in range(steps):
        loads[b].wait()
        pieces = []
        for at in range(b * per, (b + 1) * per, side):
            mark = rows_ref[at, parts * capacity :, :].astype(F32)
            for k in range(1, side):
                mark = jnp.where(lane < k * capacity, mark, rows_ref[at + k, parts * capacity :, :].astype(F32))
            mark = jnp.concatenate([mark] * (16 // MARKS), axis=0).astype(BF16)
            pieces.append(jnp.where(ids == mark[None], one, zero).reshape(nodes, LANES))
        table = jnp.concatenate(pieces, axis=1)
        near = lax.dot_general(table, q_ref[...], (((0,), (0,)), ((), ())), preferred_element_type=F32)
        joined = []
        for j in range(parts):
            rows = rows_ref[b * per : (b + 1) * per, j * capacity : (j + 1) * capacity, :].reshape(per * capacity, LANES)
            joined.append(silu_of_half((rows.astype(F32) + near[:, j * LANES : (j + 1) * LANES]).astype(BF16)))
        total += jnp.dot(table, jnp.concatenate(joined, axis=1), preferred_element_type=F32)
    update = silu(jnp.dot(total.astype(BF16), w_sum[...], preferred_element_type=F32))
    out = (first_ref[...].astype(F32) + gain[...] * layer_norm(update)).astype(BF16)
    mesh_ref[...] = out
    copy = pltpu.make_async_copy(mesh_ref, mesh_hbm, out_sem)
    copy.start()
    dec_ref[...] = jnp.dot(out, w_dec[...], preferred_element_type=F32).astype(BF16)
    copy.wait()


def edge_stage(rows, q, first, w_sum, w_dec, gain):
    nodes, latent = first.shape
    per = 16
    out = jax.ShapeDtypeStruct((nodes, latent), BF16)
    return pl.pallas_call(
        functools.partial(edge_kernel, per=per),
        out_shape=(out, out),
        in_specs=[whole(HBM)] + [whole()] * 5,
        out_specs=(whole(HBM), whole()),
        scratch_shapes=[
            pltpu.VMEM(rows.shape, BF16),
            pltpu.VMEM((nodes, latent), BF16),
            pltpu.SemaphoreType.DMA((rows.shape[0] // per,)),
            pltpu.SemaphoreType.DMA,
        ],
        compiler_params=pltpu.CompilerParams(vmem_limit_bytes=EDGE_MIB * MIB),
        name="mesh_edges",
    )(rows, q, first, w_sum, w_dec, gain.reshape(1, latent))


def pick_table(picks, tiles, nodes):
    rows, count = picks.shape[0], picks.shape[1] // 2
    ids = lax.broadcasted_iota(jnp.int32, (rows, LANES), 1).astype(jnp.int16)
    slots = [jnp.broadcast_to(picks[:, k : k + 1], (rows, LANES)).astype(jnp.int32).astype(jnp.int16) for k in range(count)]
    weights = [jnp.broadcast_to(picks[:, count + k : count + k + 1], (rows, LANES)).astype(BF16) for k in range(count)]
    blocks = []
    for j in (t * nodes // LANES + n for t in tiles for n in range(nodes // LANES)):
        at = ids + jnp.int16(j * LANES)
        block = jnp.zeros((rows, LANES), BF16)
        for slot, weight in zip(slots, weights):
            block = jnp.where(slot == at, weight, block)
        blocks.append(block)
    return jnp.concatenate(blocks, axis=1)


def hold(sources, held_ref):
    @pl.when(pl.program_id(0) == 0)
    def _():
        start = 0
        for source in sources:
            held_ref[start : start + source.shape[0], :] = source[...]
            start += source.shape[0]


def first_kernel(picks_ref, *refs, tiles, inner):
    sources, (out_ref, held_ref) = refs[:-2], refs[-2:]
    hold(sources, held_ref)
    nodes = held_ref.shape[0] // len(tiles)
    for i in range(out_ref.shape[0] // inner):
        part = slice(i * inner, (i + 1) * inner)
        table = pick_table(picks_ref[part, :], tiles, nodes)
        out_ref[part, :] = jnp.dot(table, held_ref[...], preferred_element_type=F32).astype(BF16)


def first_stage(picks, tiles, sources):
    rows, latent = picks.shape[0], sources[0].shape[1]
    block = 512
    held = sum(source.shape[0] for source in sources)
    wide = pl.BlockSpec((block, latent), lambda i: (i, 0))
    return pl.pallas_call(
        functools.partial(first_kernel, tiles=tiles, inner=256),
        grid=(rows // block,),
        out_shape=jax.ShapeDtypeStruct((rows, latent), BF16),
        in_specs=[pl.BlockSpec((block, picks.shape[1]), lambda i: (i, 0))]
        + [pl.BlockSpec(source.shape, lambda i: (0, 0)) for source in sources],
        out_specs=wide,
        scratch_shapes=[pltpu.VMEM((held, latent), BF16)],
        compiler_params=pltpu.CompilerParams(vmem_limit_bytes=16 * MIB),
        cost_estimate=pl.CostEstimate(
            flops=2 * rows * held * latent, bytes_accessed=8 * rows * latent, transcendentals=0
        ),
        name="mesh_to_grid_first",
    )(picks, *sources)


def grid_kernel(picks_ref, part_ref, grid_ref, gain, *refs, inner, tiles):
    sources, (out_ref, held_ref) = refs[:-2], refs[-2:]
    hold(sources, held_ref)
    nodes = held_ref.shape[0] // len(tiles)
    for i in range(out_ref.shape[0] // inner):
        part = slice(i * inner, (i + 1) * inner)
        table = pick_table(picks_ref[part, :], tiles, nodes)
        half = part_ref[part, :].astype(F32) + jnp.dot(table, held_ref[...], preferred_element_type=F32)
        update = silu_of_half(half)
        out_ref[part, :] = (grid_ref[part, :].astype(F32) + gain[...] * layer_norm(update)).astype(BF16)


def grid_stage(picks, part, tiles, sources, grid_feat, gain):
    rows, latent = grid_feat.shape
    block = 512
    wide = pl.BlockSpec((block, latent), lambda i: (i, 0))
    return pl.pallas_call(
        functools.partial(grid_kernel, inner=256, tiles=tiles),
        grid=(rows // block,),
        out_shape=jax.ShapeDtypeStruct((rows, latent), BF16),
        in_specs=[
            pl.BlockSpec((block, picks.shape[1]), lambda i: (i, 0)),
            wide, wide,
            pl.BlockSpec((1, latent), lambda i: (0, 0)),
        ]
        + [pl.BlockSpec(source.shape, lambda i: (0, 0)) for source in sources],
        out_specs=wide,
        scratch_shapes=[pltpu.VMEM((sum(source.shape[0] for source in sources), latent), BF16)],
        compiler_params=pltpu.CompilerParams(vmem_limit_bytes=16 * MIB),
        name="mesh_to_grid",
    )(picks, part, grid_feat, gain.reshape(1, latent), *sources)


def swap(block, axis, first):
    size = lax.axis_size(axis)
    pairs = [(i, (i + 1 if (i % 2 == 0) == first else i - 1) % size) for i in range(size)]
    return lax.ppermute(block, axis, pairs)


def on_device(
    grid_feat, mesh_feat, g2m_src, g2m_dst, g2m_weight, mesh_src, mesh_dst, mesh_count, m2g_src, m2g_weight,
    w_in, w_enc, w_send, w_recv, w_edge, w_node, w_dec, w_out, gain_enc, gain_node, gain_out,
):
    grid_rows, latent = grid_feat.shape
    nodes = mesh_feat.shape[0]
    lon_count = lax.axis_size("lon")
    tiles = lax.axis_size("lat") * lon_count
    band = lax.axis_index("lat")
    sector = lax.axis_index("lon")
    tile = band * lon_count + sector

    near_ab, near, far_a, far_b, far, own_ab, own = scatter(g2m_src, g2m_dst, g2m_weight, grid_feat, w_in, nodes, lon_count)
    from_far_a, from_far_b = swap(far_a, "lon", False), swap(far_b, "lon", False)
    from_near_ab = swap(near_ab, "lon", True)
    from_far = swap(far, "lon", False)
    from_near = swap(near, "lon", True)

    capacity = mesh_src.shape[2]
    live = lax.broadcasted_iota(jnp.int32, (tiles, capacity), 1) < mesh_count[0][:, None]
    marks = jnp.where(live, mesh_dst[0] & (nodes - 1), nodes).astype(F32)
    marks = jnp.tile(marks, (1, LANES // capacity))

    own_a, own_b = add_near(own_ab, from_near_ab)
    to_a, to_b = add_far(from_far_a, own_a), add_far(from_far_b, own_b)
    sums = (own, swap(to_a, "lat", True), swap(to_b, "lat", False), from_far, from_near)

    first, q, rows = node_stage(
        mesh_src[0] - tile * nodes, marks, sums, mesh_feat, w_enc, w_send, w_recv, gain_enc
    )
    rows_in = lax.all_to_all(rows, ("lat", "lon"), split_axis=0, concat_axis=0, tiled=True)

    m2g_src, m2g_weight, first, w_edge, w_dec = lax.optimization_barrier((m2g_src, m2g_weight, first, w_edge, w_dec))
    shift = nodes.bit_length() - 1
    index = around_index(lax.shift_right_logical(m2g_src, shift), band, sector, lon_count)
    slots = index * nodes + (m2g_src & (nodes - 1))
    columns, weights = [slots[:, k] for k in range(slots.shape[1])], [m2g_weight[:, k] for k in range(slots.shape[1])]
    for i in range(len(columns)):
        for j in range(i + 1, len(columns)):
            same = columns[i] == columns[j]
            weights[i] = weights[i] + jnp.where(same, weights[j], 0.0)
            columns[j] = jnp.where(same, -1 - j, columns[j])
    picks = jnp.stack([c.astype(F32) for c in columns] + weights, axis=1)
    edge_node = jnp.dot(w_edge, w_node, preferred_element_type=F32).astype(BF16)
    dec_out = (0.5 * jnp.dot(w_dec, w_out, preferred_element_type=F32)).astype(BF16)
    rows_in, picks, edge_node, dec_out = lax.optimization_barrier((rows_in, picks, edge_node, dec_out))

    mesh_out, decoded = edge_stage(rows_in, q, first, edge_node, dec_out, gain_node)

    from_a, from_b = swap(decoded, "lat", True), swap(decoded, "lat", False)
    far, near = swap(decoded, "lon", False), swap(decoded, "lon", True)
    corners = [swap(v, "lon", first) for v in (from_a, from_b) for first in (False, True)]
    part = first_stage(picks, (A, B, OWN), (from_a, from_b, decoded))
    grid_out = grid_stage(
        picks, part, (FAR_A, NEAR_A, FAR_B, NEAR_B, FAR, NEAR), (*corners, far, near), grid_feat, gain_out
    )
    return (grid_out, mesh_out)


def solution(mesh):
    tile = ("lat", "lon")
    rows, flat, cube = P(tile, None), P(tile), P(tile, None, None)
    return jax.shard_map(
        on_device,
        mesh=mesh,
        in_specs=(rows, rows, flat, flat, flat, cube, cube, rows, rows, rows) + (P(),) * 11,
        out_specs=(rows, rows),
        check_vma=False,
    )
```

```python
import functools

import jax
import jax.numpy as jnp
from jax import lax
from jax.experimental import pallas as pl
from jax.experimental.pallas import tpu as pltpu
from jax.sharding import PartitionSpec as P

BF16 = jnp.bfloat16
F32 = jnp.float32
LANES = 128
MARKS = 8
MIB = 1024 * 1024
EDGE_MIB = 24
NODE_MIB = 57
VMEM = pltpu.VMEM
SMEM = pltpu.SMEM
HBM = pltpu.HBM


def silu_of_half(half):
    return half + half * jnp.tanh(half)


def silu(v):
    half = v * jnp.asarray(0.5, v.dtype)
    return half + half * jnp.tanh(half)


def layer_norm(values):
    center = values - jnp.mean(values, axis=-1, keepdims=True)
    spread = jnp.mean(center * center, axis=-1, keepdims=True)
    return center * lax.rsqrt(spread + 1e-05)


def whole(space=VMEM):
    return pl.BlockSpec(memory_space=space)


NEAR_A, NEAR_B, NEAR, FAR_A, FAR_B, FAR, A, B, OWN = range(9)
BY_PLACE = (NEAR_A, NEAR, NEAR_B, A, OWN, B, FAR_A, FAR, FAR_B)


def around_index(owner, band, sector, lon_count):
    step_lat = lax.shift_right_logical(owner, lon_count.bit_length() - 1) - band
    step_lon = ((owner - sector + 1) & (lon_count - 1)) - 1
    lat_at = 1 + step_lat * (2 * (band & 1) - 1)
    lon_at = 1 + step_lon * (2 * (sector & 1) - 1)
    place = lon_at * 3 + lat_at
    index = jnp.zeros_like(place)
    for at, tile in enumerate(BY_PLACE):
        if tile:
            index = jnp.where(place == at, tile, index)
    return index


def scatter_kernel(src_hbm, dst_hbm, wgt_hbm, grid_hbm, w_hbm, *refs, nodes, lon_count):
    count = len(refs) - 17
    outs = refs[:count]
    accs = refs[count : count + 4]
    y_ref, stage_ref, grid_ref, w_ref, wide_ref, src_v, dst_v, wgt_v, src_s, dst_s, grid_sem, out_sem, sem = refs[count + 4 :]
    rows, latent = grid_ref.shape
    parts = latent // LANES
    step = 256
    chunks = rows // step

    def grid_copy(i):
        part = pl.ds(pl.multiple_of(i * step, step), step)
        return pltpu.make_async_copy(grid_hbm.at[part], grid_ref.at[part], grid_sem.at[i])

    w_in = pltpu.make_async_copy(w_hbm, w_ref, sem.at[3])
    src_in = pltpu.make_async_copy(src_hbm, src_v, sem.at[0])
    dst_in = pltpu.make_async_copy(dst_hbm, dst_v, sem.at[1])
    wgt_in = pltpu.make_async_copy(wgt_hbm, wgt_v, sem.at[2])
    src_out = pltpu.make_async_copy(src_v, src_s, sem.at[4])
    dst_out = pltpu.make_async_copy(dst_v, dst_s, sem.at[5])
    for copy in (wgt_in, w_in, grid_copy(0), src_in, dst_in):
        copy.start()
    for i in range(1, chunks):
        grid_copy(i).start()
    lines, width = src_s.shape
    wgt_in.wait()
    turned = jnp.transpose(wgt_v[...])
    for i in range(lines):
        wide_ref[i * width : (i + 1) * width, :] = jnp.broadcast_to(turned[:, i : i + 1], (width, LANES))
    w_in.wait()

    span = accs[0].shape[0] // chunks
    zero = jnp.zeros((span, LANES), F32)

    def project(i, carry):
        grid_copy(i).wait()
        base = pl.multiple_of(i * step, step)
        y = silu(jnp.dot(grid_ref[pl.ds(base, step), :], w_ref[...], preferred_element_type=F32))
        for j in range(parts):
            y_ref[pl.ds(base * parts + j, step, stride=parts), :] = y[:, j * LANES : (j + 1) * LANES]
        for acc in accs:
            acc[pl.ds(pl.multiple_of(i * span, span), span), :] = zero
        return carry

    project(0, 0)
    band, sector = lax.axis_index("lat"), lax.axis_index("lon")
    src_in.wait()
    src_v[...] = (src_v[...] - (band * lon_count + sector) * rows) * parts
    src_out.start()
    dst_in.wait()
    dst = dst_v[...]
    index = around_index(lax.shift_right_logical(dst, nodes.bit_length() - 1), band, sector, lon_count)
    dst_v[...] = (index * nodes + (dst & (nodes - 1))) * parts
    dst_out.start()
    lax.fori_loop(1, chunks, project, 0)
    src_out.wait()
    dst_out.wait()

    count = len(accs)

    def add_edges(i, carry):
        for u in range(0, width, count):
            places, sums = [], []
            for n, acc in enumerate(accs):
                s = pl.multiple_of(src_s[i, u + n], parts)
                d = pl.multiple_of(dst_s[i, u + n], parts)
                places.append(d)
                w = wide_ref[pl.ds(i * width + u + n, 1), :]
                sums.append(acc[pl.ds(d, parts), :] + w * y_ref[pl.ds(s, parts), :])
            for acc, d, total in zip(accs, places, sums):
                acc[pl.ds(d, parts), :] = total
        return carry

    lax.fori_loop(0, lines, add_edges, 0)

    def emit(i, carry):
        base = pl.multiple_of(i * step, step)
        for j in range(parts):
            rows_j = pl.ds(base * parts + j, step, stride=parts)
            total = (accs[0][rows_j, :] + accs[1][rows_j, :]) + (accs[2][rows_j, :] + accs[3][rows_j, :])
            stage_ref[pl.ds(base, step), j * LANES : (j + 1) * LANES] = total.astype(stage_ref.dtype)
        return carry

    copies, start = [], 0
    for n, out in enumerate(outs):
        per = out.shape[0]
        lax.fori_loop(start // step, (start + per) // step, emit, 0)
        copies.append(pltpu.make_async_copy(stage_ref.at[start : start + per], out, out_sem.at[n]))
        copies[-1].start()
        start += per
    for copy in copies:
        copy.wait()


def scatter(src, dst, weight, grid_feat, w_in, nodes, lon_count):
    rows, latent = grid_feat.shape
    parts = latent // LANES
    slots = 9 * nodes
    lines = src.shape[0] // LANES
    outs = tuple(jax.ShapeDtypeStruct((n * nodes, latent), BF16) for n in (2, 1, 1, 1, 1, 2, 1))
    ints = pltpu.VMEM((lines, LANES), jnp.int32)
    return pl.pallas_call(
        functools.partial(scatter_kernel, nodes=nodes, lon_count=lon_count),
        out_shape=outs,
        in_specs=[whole(HBM)] * 5,
        out_specs=(whole(HBM),) * len(outs),
        scratch_shapes=[pltpu.VMEM((slots * parts, LANES), F32)] * 4
        + [
            pltpu.VMEM((rows * parts, LANES), F32),
            pltpu.VMEM((slots, latent), BF16),
            pltpu.VMEM((rows, latent), BF16),
            pltpu.VMEM(w_in.shape, BF16),
            pltpu.VMEM((lines * LANES, LANES), F32),
            ints,
            ints,
            pltpu.VMEM((lines, LANES), F32),
            pltpu.SMEM((lines, LANES), jnp.int32),
            pltpu.SMEM((lines, LANES), jnp.int32),
            pltpu.SemaphoreType.DMA((rows // 256,)),
            pltpu.SemaphoreType.DMA((7,)),
            pltpu.SemaphoreType.DMA((6,)),
        ],
        compiler_params=pltpu.CompilerParams(vmem_limit_bytes=60 * MIB),
        name="grid_to_mesh",
    )(*(v.reshape(lines, LANES) for v in (src, dst, weight)), grid_feat, w_in)


def add_kernel(a_ref, b_ref, *outs):
    start = 0
    for out in outs:
        part = slice(start, start + out.shape[0])
        out[...] = (a_ref[part, :].astype(F32) + b_ref[part, :].astype(F32)).astype(out.dtype)
        start += out.shape[0]


def add_near(own, near):
    out = jax.ShapeDtypeStruct((own.shape[0] // 2, own.shape[1]), F32)
    return pl.pallas_call(
        add_kernel,
        out_shape=(out, out),
        in_specs=[whole()] * 2,
        out_specs=(whole(),) * 2,
        compiler_params=pltpu.CompilerParams(vmem_limit_bytes=8 * MIB),
        name="add_near",
    )(own, near)


def add_far(far, own):
    return pl.pallas_call(
        add_kernel,
        out_shape=jax.ShapeDtypeStruct(far.shape, BF16),
        in_specs=[whole()] * 2,
        out_specs=whole(),
        compiler_params=pltpu.CompilerParams(vmem_limit_bytes=8 * MIB),
        name="add_far",
    )(far, own)


def node_kernel(*refs, pieces):
    count = pieces + 7
    sources, (first_hbm, q_hbm, rows_hbm), held = refs[:count], refs[count : count + 3], refs[count + 3 : 2 * count + 3]
    first_ref, q_ref, rows_ref, in_sem, out_sem, sem = refs[2 * count + 3 :]
    loads = [pltpu.make_async_copy(a, b, in_sem.at[n]) for n, (a, b) in enumerate(zip(sources, held))]
    for load in loads:
        load.start()
    w_enc, mesh_ref, gain, w_send, w_recv, src_ref, mark_ref = held[pieces:]
    nodes, latent = mesh_ref.shape
    capacity = (rows_ref.shape[1] - MARKS) * LANES // latent
    parts = latent // LANES
    loads[0].wait()
    pooled = held[0][...].astype(F32)
    for n in range(1, pieces):
        loads[n].wait()
        pooled += held[n][...].astype(F32)
    loads[pieces].wait()
    update = silu(jnp.dot(pooled.astype(BF16), w_enc[...], preferred_element_type=F32))
    for load in loads[pieces + 1 :]:
        load.wait()
    first = (mesh_ref[...].astype(F32) + gain[...] * layer_norm(update)).astype(BF16)
    first_ref[...] = first
    first_out = pltpu.make_async_copy(first_ref, first_hbm, out_sem.at[0])
    first_out.start()
    p = (0.5 * jnp.dot(first, w_send[...], preferred_element_type=F32)).astype(BF16)
    blocks, _, block = src_ref.shape
    per = block // capacity
    ids = lax.broadcasted_iota(jnp.int32, (nodes, block), 0)
    copies = []
    for i in range(blocks):
        table = (ids == src_ref[i]).astype(BF16)
        part = pl.ds(i * per, per)
        rows = lax.dot_general(table, p, (((0,), (0,)), ((), ())), preferred_element_type=F32).astype(BF16)
        for j in range(parts):
            rows_ref[part, j * capacity : (j + 1) * capacity, :] = rows[:, j * LANES : (j + 1) * LANES].reshape(
                per, capacity, LANES
            )
        mark = mark_ref[i * per : (i + 1) * per, :]
        rows_ref[part, parts * capacity :, :] = jnp.broadcast_to(mark[:, None, :], (per, MARKS, LANES)).astype(BF16)
        copies.append(pltpu.make_async_copy(rows_ref.at[part], rows_hbm.at[part], sem.at[i]))
        copies[-1].start()
    q_ref[...] = (0.5 * jnp.dot(first, w_recv[...], preferred_element_type=F32)).astype(BF16)
    q_out = pltpu.make_async_copy(q_ref, q_hbm, out_sem.at[1])
    q_out.start()
    for copy in (first_out, q_out, *copies):
        copy.wait()


def node_stage(src, marks, sums, mesh_feat, w_enc, w_send, w_recv, gain):
    nodes, latent = mesh_feat.shape
    tiles, capacity = src.shape
    block = 512
    steps = tiles * capacity // block
    out = jax.ShapeDtypeStruct((nodes, latent), BF16)
    sent = (tiles, capacity * latent // LANES + MARKS, LANES)
    inputs = (*sums, w_enc, mesh_feat, gain.reshape(1, latent), w_send, w_recv, src.reshape(steps, 1, block), marks)
    return pl.pallas_call(
        functools.partial(node_kernel, pieces=len(sums)),
        out_shape=(out, out, jax.ShapeDtypeStruct(sent, BF16)),
        in_specs=[whole(HBM)] * len(inputs),
        out_specs=(whole(HBM),) * 3,
        scratch_shapes=[pltpu.VMEM(v.shape, v.dtype) for v in inputs]
        + [pltpu.VMEM((nodes, latent), BF16)] * 2
        + [pltpu.VMEM(sent, BF16)]
        + [pltpu.SemaphoreType.DMA((n,)) for n in (len(inputs), 2, steps)],
        compiler_params=pltpu.CompilerParams(vmem_limit_bytes=NODE_MIB * MIB),
        name="mesh_encoder",
    )(*inputs)


def edge_kernel(rows_hbm, q_ref, first_ref, w_sum, w_dec, gain, mesh_hbm, dec_ref, rows_ref, mesh_ref, sem, out_sem, *, per):
    tiles, height, _ = rows_ref.shape
    nodes, latent = q_ref.shape
    parts = latent // LANES
    capacity = (height - MARKS) // parts
    side = LANES // capacity
    steps = tiles // per
    loads = []
    for b in range(steps):
        part = pl.ds(b * per, per)
        loads.append(pltpu.make_async_copy(rows_hbm.at[part], rows_ref.at[part], sem.at[b]))
        loads[-1].start()
    lane = lax.broadcasted_iota(jnp.int32, (MARKS, LANES), 1)
    ids = lax.broadcasted_iota(jnp.int32, (nodes // 16, 16, LANES), 0) * 16
    ids = (ids + lax.broadcasted_iota(jnp.int32, ids.shape, 1)).astype(F32).astype(BF16)
    one, zero = jnp.ones((), BF16), jnp.zeros((), BF16)
    total = jnp.zeros((nodes, latent), F32)
    for b in range(steps):
        loads[b].wait()
        pieces = []
        for at in range(b * per, (b + 1) * per, side):
            mark = rows_ref[at, parts * capacity :, :].astype(F32)
            for k in range(1, side):
                mark = jnp.where(lane < k * capacity, mark, rows_ref[at + k, parts * capacity :, :].astype(F32))
            mark = jnp.concatenate([mark] * (16 // MARKS), axis=0).astype(BF16)
            pieces.append(jnp.where(ids == mark[None], one, zero).reshape(nodes, LANES))
        table = jnp.concatenate(pieces, axis=1)
        near = lax.dot_general(table, q_ref[...], (((0,), (0,)), ((), ())), preferred_element_type=F32)
        joined = []
        for j in range(parts):
            rows = rows_ref[b * per : (b + 1) * per, j * capacity : (j + 1) * capacity, :].reshape(per * capacity, LANES)
            joined.append(silu_of_half((rows.astype(F32) + near[:, j * LANES : (j + 1) * LANES]).astype(BF16)))
        total += jnp.dot(table, jnp.concatenate(joined, axis=1), preferred_element_type=F32)
    update = silu(jnp.dot(total.astype(BF16), w_sum[...], preferred_element_type=F32))
    out = (first_ref[...].astype(F32) + gain[...] * layer_norm(update)).astype(BF16)
    mesh_ref[...] = out
    copy = pltpu.make_async_copy(mesh_ref, mesh_hbm, out_sem)
    copy.start()
    dec_ref[...] = jnp.dot(out, w_dec[...], preferred_element_type=F32).astype(BF16)
    copy.wait()


def edge_stage(rows, q, first, w_sum, w_dec, gain):
    nodes, latent = first.shape
    per = 32
    out = jax.ShapeDtypeStruct((nodes, latent), BF16)
    return pl.pallas_call(
        functools.partial(edge_kernel, per=per),
        out_shape=(out, out),
        in_specs=[whole(HBM)] + [whole()] * 5,
        out_specs=(whole(HBM), whole()),
        scratch_shapes=[
            pltpu.VMEM(rows.shape, BF16),
            pltpu.VMEM((nodes, latent), BF16),
            pltpu.SemaphoreType.DMA((rows.shape[0] // per,)),
            pltpu.SemaphoreType.DMA,
        ],
        compiler_params=pltpu.CompilerParams(vmem_limit_bytes=EDGE_MIB * MIB),
        name="mesh_edges",
    )(rows, q, first, w_sum, w_dec, gain.reshape(1, latent))


def pick_table(picks, tiles, nodes):
    rows, count = picks.shape[0], picks.shape[1] // 2
    ids = lax.broadcasted_iota(jnp.int32, (rows, LANES), 1).astype(jnp.int16)
    slots = [jnp.broadcast_to(picks[:, k : k + 1], (rows, LANES)).astype(jnp.int32).astype(jnp.int16) for k in range(count)]
    weights = [jnp.broadcast_to(picks[:, count + k : count + k + 1], (rows, LANES)).astype(BF16) for k in range(count)]
    blocks = []
    for j in (t * nodes // LANES + n for t in tiles for n in range(nodes // LANES)):
        at = ids + jnp.int16(j * LANES)
        block = jnp.zeros((rows, LANES), BF16)
        for slot, weight in zip(slots, weights):
            block = jnp.where(slot == at, weight, block)
        blocks.append(block)
    return jnp.concatenate(blocks, axis=1)


def hold(sources, held_ref):
    @pl.when(pl.program_id(0) == 0)
    def _():
        start = 0
        for source in sources:
            held_ref[start : start + source.shape[0], :] = source[...]
            start += source.shape[0]


def first_kernel(picks_ref, *refs, tiles, inner):
    sources, (out_ref, held_ref) = refs[:-2], refs[-2:]
    hold(sources, held_ref)
    nodes = held_ref.shape[0] // len(tiles)
    for i in range(out_ref.shape[0] // inner):
        part = slice(i * inner, (i + 1) * inner)
        table = pick_table(picks_ref[part, :], tiles, nodes)
        out_ref[part, :] = jnp.dot(table, held_ref[...], preferred_element_type=F32).astype(BF16)


def first_stage(picks, tiles, sources):
    rows, latent = picks.shape[0], sources[0].shape[1]
    block = 512
    held = sum(source.shape[0] for source in sources)
    wide = pl.BlockSpec((block, latent), lambda i: (i, 0))
    return pl.pallas_call(
        functools.partial(first_kernel, tiles=tiles, inner=256),
        grid=(rows // block,),
        out_shape=jax.ShapeDtypeStruct((rows, latent), BF16),
        in_specs=[pl.BlockSpec((block, picks.shape[1]), lambda i: (i, 0))]
        + [pl.BlockSpec(source.shape, lambda i: (0, 0)) for source in sources],
        out_specs=wide,
        scratch_shapes=[pltpu.VMEM((held, latent), BF16)],
        compiler_params=pltpu.CompilerParams(vmem_limit_bytes=16 * MIB),
        cost_estimate=pl.CostEstimate(
            flops=2 * rows * held * latent, bytes_accessed=8 * rows * latent, transcendentals=0
        ),
        name="mesh_to_grid_first",
    )(picks, *sources)


def grid_kernel(picks_ref, part_ref, grid_ref, gain, *refs, inner, tiles):
    sources, (out_ref, held_ref) = refs[:-2], refs[-2:]
    hold(sources, held_ref)
    nodes = held_ref.shape[0] // len(tiles)
    for i in range(out_ref.shape[0] // inner):
        part = slice(i * inner, (i + 1) * inner)
        table = pick_table(picks_ref[part, :], tiles, nodes)
        half = part_ref[part, :].astype(F32) + jnp.dot(table, held_ref[...], preferred_element_type=F32)
        update = silu_of_half(half)
        out_ref[part, :] = (grid_ref[part, :].astype(F32) + gain[...] * layer_norm(update)).astype(BF16)


def grid_stage(picks, part, tiles, sources, grid_feat, gain):
    rows, latent = grid_feat.shape
    block = 512
    wide = pl.BlockSpec((block, latent), lambda i: (i, 0))
    return pl.pallas_call(
        functools.partial(grid_kernel, inner=256, tiles=tiles),
        grid=(rows // block,),
        out_shape=jax.ShapeDtypeStruct((rows, latent), BF16),
        in_specs=[
            pl.BlockSpec((block, picks.shape[1]), lambda i: (i, 0)),
            wide, wide,
            pl.BlockSpec((1, latent), lambda i: (0, 0)),
        ]
        + [pl.BlockSpec(source.shape, lambda i: (0, 0)) for source in sources],
        out_specs=wide,
        scratch_shapes=[pltpu.VMEM((sum(source.shape[0] for source in sources), latent), BF16)],
        compiler_params=pltpu.CompilerParams(vmem_limit_bytes=16 * MIB),
        name="mesh_to_grid",
    )(picks, part, grid_feat, gain.reshape(1, latent), *sources)


def swap(block, axis, first):
    size = lax.axis_size(axis)
    pairs = [(i, (i + 1 if (i % 2 == 0) == first else i - 1) % size) for i in range(size)]
    return lax.ppermute(block, axis, pairs)


def on_device(
    grid_feat, mesh_feat, g2m_src, g2m_dst, g2m_weight, mesh_src, mesh_dst, mesh_count, m2g_src, m2g_weight,
    w_in, w_enc, w_send, w_recv, w_edge, w_node, w_dec, w_out, gain_enc, gain_node, gain_out,
):
    grid_rows, latent = grid_feat.shape
    nodes = mesh_feat.shape[0]
    lon_count = lax.axis_size("lon")
    tiles = lax.axis_size("lat") * lon_count
    band = lax.axis_index("lat")
    sector = lax.axis_index("lon")
    tile = band * lon_count + sector

    near_ab, near, far_a, far_b, far, own_ab, own = scatter(g2m_src, g2m_dst, g2m_weight, grid_feat, w_in, nodes, lon_count)
    from_far_a, from_far_b = swap(far_a, "lon", False), swap(far_b, "lon", False)
    from_near_ab = swap(near_ab, "lon", True)
    from_far = swap(far, "lon", False)
    from_near = swap(near, "lon", True)

    capacity = mesh_src.shape[2]
    live = lax.broadcasted_iota(jnp.int32, (tiles, capacity), 1) < mesh_count[0][:, None]
    marks = jnp.where(live, mesh_dst[0] & (nodes - 1), nodes).astype(F32)
    marks = jnp.tile(marks, (1, LANES // capacity))

    own_a, own_b = add_near(own_ab, from_near_ab)
    to_a, to_b = add_far(from_far_a, own_a), add_far(from_far_b, own_b)
    sums = (own, swap(to_a, "lat", True), swap(to_b, "lat", False), from_far, from_near)

    first, q, rows = node_stage(
        mesh_src[0] - tile * nodes, marks, sums, mesh_feat, w_enc, w_send, w_recv, gain_enc
    )
    rows_in = lax.all_to_all(rows, ("lat", "lon"), split_axis=0, concat_axis=0, tiled=True)

    m2g_src, m2g_weight, first, w_edge, w_dec = lax.optimization_barrier((m2g_src, m2g_weight, first, w_edge, w_dec))
    shift = nodes.bit_length() - 1
    index = around_index(lax.shift_right_logical(m2g_src, shift), band, sector, lon_count)
    slots = index * nodes + (m2g_src & (nodes - 1))
    columns, weights = [slots[:, k] for k in range(slots.shape[1])], [m2g_weight[:, k] for k in range(slots.shape[1])]
    for i in range(len(columns)):
        for j in range(i + 1, len(columns)):
            same = columns[i] == columns[j]
            weights[i] = weights[i] + jnp.where(same, weights[j], 0.0)
            columns[j] = jnp.where(same, -1 - j, columns[j])
    picks = jnp.stack([c.astype(F32) for c in columns] + weights, axis=1)
    edge_node = jnp.dot(w_edge, w_node, preferred_element_type=F32).astype(BF16)
    dec_out = (0.5 * jnp.dot(w_dec, w_out, preferred_element_type=F32)).astype(BF16)
    rows_in, picks, edge_node, dec_out = lax.optimization_barrier((rows_in, picks, edge_node, dec_out))

    mesh_out, decoded = edge_stage(rows_in, q, first, edge_node, dec_out, gain_node)

    from_a, from_b = swap(decoded, "lat", True), swap(decoded, "lat", False)
    far, near = swap(decoded, "lon", False), swap(decoded, "lon", True)
    corners = [swap(v, "lon", first) for v in (from_a, from_b) for first in (False, True)]
    part = first_stage(picks, (A, B, OWN), (from_a, from_b, decoded))
    grid_out = grid_stage(
        picks, part, (FAR_A, NEAR_A, FAR_B, NEAR_B, FAR, NEAR), (*corners, far, near), grid_feat, gain_out
    )
    return (grid_out, mesh_out)


def solution(mesh):
    tile = ("lat", "lon")
    rows, flat, cube = P(tile, None), P(tile), P(tile, None, None)
    return jax.shard_map(
        on_device,
        mesh=mesh,
        in_specs=(rows, rows, flat, flat, flat, cube, cube, rows, rows, rows) + (P(),) * 11,
        out_specs=(rows, rows),
        check_vma=False,
    )
```

```python
import functools

import jax
import jax.numpy as jnp
from jax import lax
from jax.experimental import pallas as pl
from jax.experimental.pallas import tpu as pltpu
from jax.sharding import PartitionSpec as P

BF16 = jnp.bfloat16
F32 = jnp.float32
LANES = 128
MARKS = 16
MIB = 1024 * 1024
EDGE_MIB = 24
NODE_MIB = 57
VMEM = pltpu.VMEM
SMEM = pltpu.SMEM
HBM = pltpu.HBM


def silu_of_half(half):
    return half + half * jnp.tanh(half)


def silu(v):
    half = v * jnp.asarray(0.5, v.dtype)
    return half + half * jnp.tanh(half)


def layer_norm(values):
    center = values - jnp.mean(values, axis=-1, keepdims=True)
    spread = jnp.mean(center * center, axis=-1, keepdims=True)
    return center * lax.rsqrt(spread + 1e-05)


def whole(space=VMEM):
    return pl.BlockSpec(memory_space=space)


NEAR_A, NEAR_B, NEAR, FAR_A, FAR_B, FAR, A, B, OWN = range(9)
BY_PLACE = (NEAR_A, NEAR, NEAR_B, A, OWN, B, FAR_A, FAR, FAR_B)


def around_index(owner, band, sector, lon_count):
    step_lat = lax.shift_right_logical(owner, lon_count.bit_length() - 1) - band
    step_lon = ((owner - sector + 1) & (lon_count - 1)) - 1
    lat_at = 1 + step_lat * (2 * (band & 1) - 1)
    lon_at = 1 + step_lon * (2 * (sector & 1) - 1)
    place = lon_at * 3 + lat_at
    index = jnp.zeros_like(place)
    for at, tile in enumerate(BY_PLACE):
        if tile:
            index = jnp.where(place == at, tile, index)
    return index


def scatter_kernel(src_hbm, dst_hbm, wgt_hbm, grid_hbm, w_hbm, *refs, nodes, lon_count):
    count = len(refs) - 17
    outs = refs[:count]
    accs = refs[count : count + 4]
    y_ref, stage_ref, grid_ref, w_ref, wide_ref, src_v, dst_v, wgt_v, src_s, dst_s, grid_sem, out_sem, sem = refs[count + 4 :]
    rows, latent = grid_ref.shape
    parts = latent // LANES
    step = 256
    chunks = rows // step

    def grid_copy(i):
        part = pl.ds(pl.multiple_of(i * step, step), step)
        return pltpu.make_async_copy(grid_hbm.at[part], grid_ref.at[part], grid_sem.at[i])

    w_in = pltpu.make_async_copy(w_hbm, w_ref, sem.at[3])
    src_in = pltpu.make_async_copy(src_hbm, src_v, sem.at[0])
    dst_in = pltpu.make_async_copy(dst_hbm, dst_v, sem.at[1])
    wgt_in = pltpu.make_async_copy(wgt_hbm, wgt_v, sem.at[2])
    src_out = pltpu.make_async_copy(src_v, src_s, sem.at[4])
    dst_out = pltpu.make_async_copy(dst_v, dst_s, sem.at[5])
    for copy in (wgt_in, w_in, grid_copy(0), src_in, dst_in):
        copy.start()
    for i in range(1, chunks):
        grid_copy(i).start()
    lines, width = src_s.shape
    wgt_in.wait()
    turned = jnp.transpose(wgt_v[...])
    for i in range(lines):
        wide_ref[i * width : (i + 1) * width, :] = jnp.broadcast_to(turned[:, i : i + 1], (width, LANES))
    w_in.wait()

    span = accs[0].shape[0] // chunks
    zero = jnp.zeros((span, LANES), F32)

    def project(i, carry):
        grid_copy(i).wait()
        base = pl.multiple_of(i * step, step)
        y = silu(jnp.dot(grid_ref[pl.ds(base, step), :], w_ref[...], preferred_element_type=F32))
        for j in range(parts):
            y_ref[pl.ds(base * parts + j, step, stride=parts), :] = y[:, j * LANES : (j + 1) * LANES]
        for acc in accs:
            acc[pl.ds(pl.multiple_of(i * span, span), span), :] = zero
        return carry

    project(0, 0)
    band, sector = lax.axis_index("lat"), lax.axis_index("lon")
    src_in.wait()
    src_v[...] = (src_v[...] - (band * lon_count + sector) * rows) * parts
    src_out.start()
    dst_in.wait()
    dst = dst_v[...]
    index = around_index(lax.shift_right_logical(dst, nodes.bit_length() - 1), band, sector, lon_count)
    dst_v[...] = (index * nodes + (dst & (nodes - 1))) * parts
    dst_out.start()
    lax.fori_loop(1, chunks, project, 0)
    src_out.wait()
    dst_out.wait()

    count = len(accs)

    def add_edges(i, carry):
        for u in range(0, width, count):
            places, sums = [], []
            for n, acc in enumerate(accs):
                s = pl.multiple_of(src_s[i, u + n], parts)
                d = pl.multiple_of(dst_s[i, u + n], parts)
                places.append(d)
                w = wide_ref[pl.ds(i * width + u + n, 1), :]
                sums.append(acc[pl.ds(d, parts), :] + w * y_ref[pl.ds(s, parts), :])
            for acc, d, total in zip(accs, places, sums):
                acc[pl.ds(d, parts), :] = total
        return carry

    lax.fori_loop(0, lines, add_edges, 0)

    def emit(i, carry):
        base = pl.multiple_of(i * step, step)
        for j in range(parts):
            rows_j = pl.ds(base * parts + j, step, stride=parts)
            total = (accs[0][rows_j, :] + accs[1][rows_j, :]) + (accs[2][rows_j, :] + accs[3][rows_j, :])
            stage_ref[pl.ds(base, step), j * LANES : (j + 1) * LANES] = total.astype(stage_ref.dtype)
        return carry

    copies, start = [], 0
    for n, out in enumerate(outs):
        per = out.shape[0]
        lax.fori_loop(start // step, (start + per) // step, emit, 0)
        copies.append(pltpu.make_async_copy(stage_ref.at[start : start + per], out, out_sem.at[n]))
        copies[-1].start()
        start += per
    for copy in copies:
        copy.wait()


def scatter(src, dst, weight, grid_feat, w_in, nodes, lon_count):
    rows, latent = grid_feat.shape
    parts = latent // LANES
    slots = 9 * nodes
    lines = src.shape[0] // LANES
    outs = tuple(jax.ShapeDtypeStruct((n * nodes, latent), BF16) for n in (2, 1, 1, 1, 1, 2, 1))
    ints = pltpu.VMEM((lines, LANES), jnp.int32)
    return pl.pallas_call(
        functools.partial(scatter_kernel, nodes=nodes, lon_count=lon_count),
        out_shape=outs,
        in_specs=[whole(HBM)] * 5,
        out_specs=(whole(HBM),) * len(outs),
        scratch_shapes=[pltpu.VMEM((slots * parts, LANES), F32)] * 4
        + [
            pltpu.VMEM((rows * parts, LANES), F32),
            pltpu.VMEM((slots, latent), BF16),
            pltpu.VMEM((rows, latent), BF16),
            pltpu.VMEM(w_in.shape, BF16),
            pltpu.VMEM((lines * LANES, LANES), F32),
            ints,
            ints,
            pltpu.VMEM((lines, LANES), F32),
            pltpu.SMEM((lines, LANES), jnp.int32),
            pltpu.SMEM((lines, LANES), jnp.int32),
            pltpu.SemaphoreType.DMA((rows // 256,)),
            pltpu.SemaphoreType.DMA((7,)),
            pltpu.SemaphoreType.DMA((6,)),
        ],
        compiler_params=pltpu.CompilerParams(vmem_limit_bytes=60 * MIB),
        name="grid_to_mesh",
    )(*(v.reshape(lines, LANES) for v in (src, dst, weight)), grid_feat, w_in)


def add_kernel(a_ref, b_ref, *outs):
    start = 0
    for out in outs:
        part = slice(start, start + out.shape[0])
        out[...] = (a_ref[part, :].astype(F32) + b_ref[part, :].astype(F32)).astype(out.dtype)
        start += out.shape[0]


def add_near(own, near):
    out = jax.ShapeDtypeStruct((own.shape[0] // 2, own.shape[1]), F32)
    return pl.pallas_call(
        add_kernel,
        out_shape=(out, out),
        in_specs=[whole()] * 2,
        out_specs=(whole(),) * 2,
        compiler_params=pltpu.CompilerParams(vmem_limit_bytes=8 * MIB),
        name="add_near",
    )(own, near)


def add_far(far, own):
    return pl.pallas_call(
        add_kernel,
        out_shape=jax.ShapeDtypeStruct(far.shape, BF16),
        in_specs=[whole()] * 2,
        out_specs=whole(),
        compiler_params=pltpu.CompilerParams(vmem_limit_bytes=8 * MIB),
        name="add_far",
    )(far, own)


def node_kernel(*refs, pieces):
    count = pieces + 7
    sources, (first_hbm, q_hbm, rows_hbm), held = refs[:count], refs[count : count + 3], refs[count + 3 : 2 * count + 3]
    first_ref, q_ref, rows_ref, in_sem, out_sem, sem = refs[2 * count + 3 :]
    loads = [pltpu.make_async_copy(a, b, in_sem.at[n]) for n, (a, b) in enumerate(zip(sources, held))]
    for load in loads:
        load.start()
    w_enc, mesh_ref, gain, w_send, w_recv, src_ref, mark_ref = held[pieces:]
    nodes, latent = mesh_ref.shape
    capacity = (rows_ref.shape[1] - MARKS) * LANES // latent
    parts = latent // LANES
    loads[0].wait()
    pooled = held[0][...].astype(F32)
    for n in range(1, pieces):
        loads[n].wait()
        pooled += held[n][...].astype(F32)
    loads[pieces].wait()
    update = silu(jnp.dot(pooled.astype(BF16), w_enc[...], preferred_element_type=F32))
    for load in loads[pieces + 1 :]:
        load.wait()
    first = (mesh_ref[...].astype(F32) + gain[...] * layer_norm(update)).astype(BF16)
    first_ref[...] = first
    first_out = pltpu.make_async_copy(first_ref, first_hbm, out_sem.at[0])
    first_out.start()
    p = (0.5 * jnp.dot(first, w_send[...], preferred_element_type=F32)).astype(BF16)
    blocks, _, block = src_ref.shape
    per = block // capacity
    ids = lax.broadcasted_iota(jnp.int32, (nodes, block), 0)
    copies = []
    for i in range(blocks):
        table = (ids == src_ref[i]).astype(BF16)
        part = pl.ds(i * per, per)
        rows = lax.dot_general(table, p, (((0,), (0,)), ((), ())), preferred_element_type=F32).astype(BF16)
        for j in range(parts):
            rows_ref[part, j * capacity : (j + 1) * capacity, :] = rows[:, j * LANES : (j + 1) * LANES].reshape(
                per, capacity, LANES
            )
        mark = mark_ref[i * per : (i + 1) * per, :]
        rows_ref[part, parts * capacity :, :] = jnp.broadcast_to(mark[:, None, :], (per, MARKS, LANES)).astype(BF16)
        copies.append(pltpu.make_async_copy(rows_ref.at[part], rows_hbm.at[part], sem.at[i]))
        copies[-1].start()
    q_ref[...] = (0.5 * jnp.dot(first, w_recv[...], preferred_element_type=F32)).astype(BF16)
    q_out = pltpu.make_async_copy(q_ref, q_hbm, out_sem.at[1])
    q_out.start()
    for copy in (first_out, q_out, *copies):
        copy.wait()


def node_stage(src, marks, sums, mesh_feat, w_enc, w_send, w_recv, gain):
    nodes, latent = mesh_feat.shape
    tiles, capacity = src.shape
    block = 512
    steps = tiles * capacity // block
    out = jax.ShapeDtypeStruct((nodes, latent), BF16)
    sent = (tiles, capacity * latent // LANES + MARKS, LANES)
    inputs = (*sums, w_enc, mesh_feat, gain.reshape(1, latent), w_send, w_recv, src.reshape(steps, 1, block), marks)
    return pl.pallas_call(
        functools.partial(node_kernel, pieces=len(sums)),
        out_shape=(out, out, jax.ShapeDtypeStruct(sent, BF16)),
        in_specs=[whole(HBM)] * len(inputs),
        out_specs=(whole(HBM),) * 3,
        scratch_shapes=[pltpu.VMEM(v.shape, v.dtype) for v in inputs]
        + [pltpu.VMEM((nodes, latent), BF16)] * 2
        + [pltpu.VMEM(sent, BF16)]
        + [pltpu.SemaphoreType.DMA((n,)) for n in (len(inputs), 2, steps)],
        compiler_params=pltpu.CompilerParams(vmem_limit_bytes=NODE_MIB * MIB),
        name="mesh_encoder",
    )(*inputs)


def edge_kernel(rows_hbm, q_ref, first_ref, w_sum, w_dec, gain, mesh_hbm, dec_ref, rows_ref, mesh_ref, sem, out_sem, *, per):
    tiles, height, _ = rows_ref.shape
    nodes, latent = q_ref.shape
    parts = latent // LANES
    capacity = (height - MARKS) // parts
    side = LANES // capacity
    steps = tiles // per
    loads = []
    for b in range(steps):
        part = pl.ds(b * per, per)
        loads.append(pltpu.make_async_copy(rows_hbm.at[part], rows_ref.at[part], sem.at[b]))
        loads[-1].start()
    lane = lax.broadcasted_iota(jnp.int32, (MARKS, LANES), 1)
    ids = lax.broadcasted_iota(jnp.int32, (nodes // 16, 16, LANES), 0) * 16
    ids = (ids + lax.broadcasted_iota(jnp.int32, ids.shape, 1)).astype(F32).astype(BF16)
    one, zero = jnp.ones((), BF16), jnp.zeros((), BF16)
    total = jnp.zeros((nodes, latent), F32)
    for b in range(steps):
        loads[b].wait()
        pieces = []
        for at in range(b * per, (b + 1) * per, side):
            mark = rows_ref[at, parts * capacity :, :].astype(F32)
            for k in range(1, side):
                mark = jnp.where(lane < k * capacity, mark, rows_ref[at + k, parts * capacity :, :].astype(F32))
            mark = jnp.concatenate([mark] * (16 // MARKS), axis=0).astype(BF16)
            pieces.append(jnp.where(ids == mark[None], one, zero).reshape(nodes, LANES))
        table = jnp.concatenate(pieces, axis=1)
        near = lax.dot_general(table, q_ref[...], (((0,), (0,)), ((), ())), preferred_element_type=F32)
        joined = []
        for j in range(parts):
            rows = rows_ref[b * per : (b + 1) * per, j * capacity : (j + 1) * capacity, :].reshape(per * capacity, LANES)
            joined.append(silu_of_half((rows.astype(F32) + near[:, j * LANES : (j + 1) * LANES]).astype(BF16)))
        total += jnp.dot(table, jnp.concatenate(joined, axis=1), preferred_element_type=F32)
    update = silu(jnp.dot(total.astype(BF16), w_sum[...], preferred_element_type=F32))
    out = (first_ref[...].astype(F32) + gain[...] * layer_norm(update)).astype(BF16)
    mesh_ref[...] = out
    copy = pltpu.make_async_copy(mesh_ref, mesh_hbm, out_sem)
    copy.start()
    dec_ref[...] = jnp.dot(out, w_dec[...], preferred_element_type=F32).astype(BF16)
    copy.wait()


def edge_stage(rows, q, first, w_sum, w_dec, gain):
    nodes, latent = first.shape
    per = 32
    out = jax.ShapeDtypeStruct((nodes, latent), BF16)
    return pl.pallas_call(
        functools.partial(edge_kernel, per=per),
        out_shape=(out, out),
        in_specs=[whole(HBM)] + [whole()] * 5,
        out_specs=(whole(HBM), whole()),
        scratch_shapes=[
            pltpu.VMEM(rows.shape, BF16),
            pltpu.VMEM((nodes, latent), BF16),
            pltpu.SemaphoreType.DMA((rows.shape[0] // per,)),
            pltpu.SemaphoreType.DMA,
        ],
        compiler_params=pltpu.CompilerParams(vmem_limit_bytes=EDGE_MIB * MIB),
        name="mesh_edges",
    )(rows, q, first, w_sum, w_dec, gain.reshape(1, latent))


def pick_table(picks, tiles, nodes):
    rows, count = picks.shape[0], picks.shape[1] // 2
    ids = lax.broadcasted_iota(jnp.int32, (rows, LANES), 1).astype(jnp.int16)
    slots = [jnp.broadcast_to(picks[:, k : k + 1], (rows, LANES)).astype(jnp.int32).astype(jnp.int16) for k in range(count)]
    weights = [jnp.broadcast_to(picks[:, count + k : count + k + 1], (rows, LANES)).astype(BF16) for k in range(count)]
    blocks = []
    for j in (t * nodes // LANES + n for t in tiles for n in range(nodes // LANES)):
        at = ids + jnp.int16(j * LANES)
        block = jnp.zeros((rows, LANES), BF16)
        for slot, weight in zip(slots, weights):
            block = jnp.where(slot == at, weight, block)
        blocks.append(block)
    return jnp.concatenate(blocks, axis=1)


def hold(sources, held_ref):
    @pl.when(pl.program_id(0) == 0)
    def _():
        start = 0
        for source in sources:
            held_ref[start : start + source.shape[0], :] = source[...]
            start += source.shape[0]


def first_kernel(picks_ref, *refs, tiles, inner):
    sources, (out_ref, held_ref) = refs[:-2], refs[-2:]
    hold(sources, held_ref)
    nodes = held_ref.shape[0] // len(tiles)
    for i in range(out_ref.shape[0] // inner):
        part = slice(i * inner, (i + 1) * inner)
        table = pick_table(picks_ref[part, :], tiles, nodes)
        out_ref[part, :] = jnp.dot(table, held_ref[...], preferred_element_type=F32).astype(BF16)


def first_stage(picks, tiles, sources):
    rows, latent = picks.shape[0], sources[0].shape[1]
    block = 512
    held = sum(source.shape[0] for source in sources)
    wide = pl.BlockSpec((block, latent), lambda i: (i, 0))
    return pl.pallas_call(
        functools.partial(first_kernel, tiles=tiles, inner=256),
        grid=(rows // block,),
        out_shape=jax.ShapeDtypeStruct((rows, latent), BF16),
        in_specs=[pl.BlockSpec((block, picks.shape[1]), lambda i: (i, 0))]
        + [pl.BlockSpec(source.shape, lambda i: (0, 0)) for source in sources],
        out_specs=wide,
        scratch_shapes=[pltpu.VMEM((held, latent), BF16)],
        compiler_params=pltpu.CompilerParams(vmem_limit_bytes=16 * MIB),
        cost_estimate=pl.CostEstimate(
            flops=2 * rows * held * latent, bytes_accessed=8 * rows * latent, transcendentals=0
        ),
        name="mesh_to_grid_first",
    )(picks, *sources)


def grid_kernel(picks_ref, part_ref, grid_ref, gain, *refs, inner, tiles):
    sources, (out_ref, held_ref) = refs[:-2], refs[-2:]
    hold(sources, held_ref)
    nodes = held_ref.shape[0] // len(tiles)
    for i in range(out_ref.shape[0] // inner):
        part = slice(i * inner, (i + 1) * inner)
        table = pick_table(picks_ref[part, :], tiles, nodes)
        half = part_ref[part, :].astype(F32) + jnp.dot(table, held_ref[...], preferred_element_type=F32)
        update = silu_of_half(half)
        out_ref[part, :] = (grid_ref[part, :].astype(F32) + gain[...] * layer_norm(update)).astype(BF16)


def grid_stage(picks, part, tiles, sources, grid_feat, gain):
    rows, latent = grid_feat.shape
    block = 512
    wide = pl.BlockSpec((block, latent), lambda i: (i, 0))
    return pl.pallas_call(
        functools.partial(grid_kernel, inner=256, tiles=tiles),
        grid=(rows // block,),
        out_shape=jax.ShapeDtypeStruct((rows, latent), BF16),
        in_specs=[
            pl.BlockSpec((block, picks.shape[1]), lambda i: (i, 0)),
            wide, wide,
            pl.BlockSpec((1, latent), lambda i: (0, 0)),
        ]
        + [pl.BlockSpec(source.shape, lambda i: (0, 0)) for source in sources],
        out_specs=wide,
        scratch_shapes=[pltpu.VMEM((sum(source.shape[0] for source in sources), latent), BF16)],
        compiler_params=pltpu.CompilerParams(vmem_limit_bytes=16 * MIB),
        name="mesh_to_grid",
    )(picks, part, grid_feat, gain.reshape(1, latent), *sources)


def swap(block, axis, first):
    size = lax.axis_size(axis)
    pairs = [(i, (i + 1 if (i % 2 == 0) == first else i - 1) % size) for i in range(size)]
    return lax.ppermute(block, axis, pairs)


def on_device(
    grid_feat, mesh_feat, g2m_src, g2m_dst, g2m_weight, mesh_src, mesh_dst, mesh_count, m2g_src, m2g_weight,
    w_in, w_enc, w_send, w_recv, w_edge, w_node, w_dec, w_out, gain_enc, gain_node, gain_out,
):
    grid_rows, latent = grid_feat.shape
    nodes = mesh_feat.shape[0]
    lon_count = lax.axis_size("lon")
    tiles = lax.axis_size("lat") * lon_count
    band = lax.axis_index("lat")
    sector = lax.axis_index("lon")
    tile = band * lon_count + sector

    near_ab, near, far_a, far_b, far, own_ab, own = scatter(g2m_src, g2m_dst, g2m_weight, grid_feat, w_in, nodes, lon_count)
    from_far_a, from_far_b = swap(far_a, "lon", False), swap(far_b, "lon", False)
    from_near_ab = swap(near_ab, "lon", True)
    from_far = swap(far, "lon", False)
    from_near = swap(near, "lon", True)

    capacity = mesh_src.shape[2]
    live = lax.broadcasted_iota(jnp.int32, (tiles, capacity), 1) < mesh_count[0][:, None]
    marks = jnp.where(live, mesh_dst[0] & (nodes - 1), nodes).astype(F32)
    marks = jnp.tile(marks, (1, LANES // capacity))

    own_a, own_b = add_near(own_ab, from_near_ab)
    to_a, to_b = add_far(from_far_a, own_a), add_far(from_far_b, own_b)
    sums = (own, swap(to_a, "lat", True), swap(to_b, "lat", False), from_far, from_near)

    first, q, rows = node_stage(
        mesh_src[0] - tile * nodes, marks, sums, mesh_feat, w_enc, w_send, w_recv, gain_enc
    )
    rows_in = lax.all_to_all(rows, ("lat", "lon"), split_axis=0, concat_axis=0, tiled=True)

    m2g_src, m2g_weight, first, w_edge, w_dec = lax.optimization_barrier((m2g_src, m2g_weight, first, w_edge, w_dec))
    shift = nodes.bit_length() - 1
    index = around_index(lax.shift_right_logical(m2g_src, shift), band, sector, lon_count)
    slots = index * nodes + (m2g_src & (nodes - 1))
    columns, weights = [slots[:, k] for k in range(slots.shape[1])], [m2g_weight[:, k] for k in range(slots.shape[1])]
    for i in range(len(columns)):
        for j in range(i + 1, len(columns)):
            same = columns[i] == columns[j]
            weights[i] = weights[i] + jnp.where(same, weights[j], 0.0)
            columns[j] = jnp.where(same, -1 - j, columns[j])
    picks = jnp.stack([c.astype(F32) for c in columns] + weights, axis=1)
    edge_node = jnp.dot(w_edge, w_node, preferred_element_type=F32).astype(BF16)
    dec_out = (0.5 * jnp.dot(w_dec, w_out, preferred_element_type=F32)).astype(BF16)
    rows_in, picks, edge_node, dec_out = lax.optimization_barrier((rows_in, picks, edge_node, dec_out))

    mesh_out, decoded = edge_stage(rows_in, q, first, edge_node, dec_out, gain_node)

    from_a, from_b = swap(decoded, "lat", True), swap(decoded, "lat", False)
    far, near = swap(decoded, "lon", False), swap(decoded, "lon", True)
    corners = [swap(v, "lon", first) for v in (from_a, from_b) for first in (False, True)]
    part = first_stage(picks, (A, B, OWN), (from_a, from_b, decoded))
    grid_out = grid_stage(
        picks, part, (FAR_A, NEAR_A, FAR_B, NEAR_B, FAR, NEAR), (*corners, far, near), grid_feat, gain_out
    )
    return (grid_out, mesh_out)


def solution(mesh):
    tile = ("lat", "lon")
    rows, flat, cube = P(tile, None), P(tile), P(tile, None, None)
    return jax.shard_map(
        on_device,
        mesh=mesh,
        in_specs=(rows, rows, flat, flat, flat, cube, cube, rows, rows, rows) + (P(),) * 11,
        out_specs=(rows, rows),
        check_vma=False,
    )
```
